128 devices in a mesh: ctx: 32 (over z, y, x_lo), tp: 4 (over x_hi, core).
Axes of the slice: x: 4 (x_hi: 2, x_lo: 2; x = x_hi * 2 + x_lo), y: 4, z: 4, core: 2. Of those that a mesh axis runs over, the one named last changes fastest.
Arguments:
- tokens: bfloat16 [8192, 4096], P('ctx', 'tp'), may hold values from -7 to 7
- in_weight: bfloat16 [4096, 2, 4096], P(None, None, 'tp'), may hold values from -0.09375 to 0.09375
- short_kernel: float32 [3, 2, 4096], P(None, None, 'tp'), may hold values from -3 to 3
- long_filter: float32 [8192, 4096], P('ctx', 'tp'), may hold values from -3 to 3
- skip_gain: float32 [4096], P('tp'), may hold values from -4 to 4
Outputs:
- block_output: bfloat16 [8192, 4096], P('ctx', 'tp')
The draws below stay inside these ranges and needn't reach their ends.
All inputs are finite; a program needn't handle non-finite values.
Results may differ from the reference program's by a relative error of at most 0.007.
Values may be sent and summed in bfloat16 or wider, within the bound.
No kernel may reach another device: no remote copies, remote signals or barrier semaphores. Data moves between devices by JAX's collectives and lax.ppermute only.
A program may use at most 128 MiB of HBM per device.

```python
import math
import jax
import jax.numpy as jnp
from jax import lax

D = 4096
SHORT_TAPS = 3
NUCLEOTIDE_COUNT = 8192


def draw_tokens(key, part):
    key = jax.random.fold_in(key, 11)
    token_keys = jax.random.split(key, 2)
    noise = jnp.clip(jax.random.normal(token_keys[0], (NUCLEOTIDE_COUNT, D), jnp.float32), -5.5, 5.5)
    channel_level = jnp.clip(0.5 * jax.random.normal(token_keys[1], (D,), jnp.float32), -1.5, 1.5)
    return (noise + channel_level[None, :]).astype(jnp.bfloat16)


def draw_long_filter(key, part):
    key = jax.random.fold_in(key, 23)
    derived_prng_keys = jax.random.split(key, 8)
    window_beginnings = jnp.arange(NUCLEOTIDE_COUNT, dtype=jnp.float32)[:, None]
    slow_share = 0.5
    jitter = jnp.clip(jax.random.normal(derived_prng_keys[0], (NUCLEOTIDE_COUNT, D), jnp.float32), -5.0, 5.0)
    is_slow = jax.random.uniform(derived_prng_keys[1], (D,), jnp.float32) < slow_share
    slow_rate = jnp.exp(jax.random.uniform(derived_prng_keys[2], (D,), jnp.float32, math.log(0.1 / NUCLEOTIDE_COUNT), math.log(2.0 / NUCLEOTIDE_COUNT)))
    fast_rate = jnp.exp(jax.random.uniform(derived_prng_keys[3], (D,), jnp.float32, math.log(1.0 / 64.0), math.log(1.0 / 16.0)))
    decay_rate = jnp.where(is_slow, slow_rate, fast_rate)
    perturbation_pulses = jax.random.randint(derived_prng_keys[4], (3,), 1, NUCLEOTIDE_COUNT)
    objective_history = jax.random.uniform(derived_prng_keys[5], (3, D), jnp.float32, 0.5, 0.8)
    magnitude_multiplier = jnp.ones((NUCLEOTIDE_COUNT, D), jnp.float32)
    for perturbation_pulse in range(3):
        magnitude_multiplier = magnitude_multiplier * jnp.where(window_beginnings >= perturbation_pulses[perturbation_pulse].astype(jnp.float32), objective_history[perturbation_pulse][None, :], 1.0)
    spread = jnp.sqrt((1.0 - jnp.exp(-2.0 * decay_rate)) / (1.0 - jnp.exp(-2.0 * decay_rate * NUCLEOTIDE_COUNT)))
    floor_sign = jnp.where(jax.random.uniform(derived_prng_keys[7], (D,), jnp.float32) < 0.5, 1.0, -1.0)
    floor_level = floor_sign * jax.random.uniform(derived_prng_keys[6], (D,), jnp.float32, 0.4, 0.8) / NUCLEOTIDE_COUNT
    shaped = jitter * jnp.exp(-decay_rate[None, :] * window_beginnings) * magnitude_multiplier * spread[None, :]
    return shaped + floor_level[None, :]


def steps_of(rng, extent, cuts, smallest, high):
    factor_of = 1.0
    for axis_at, shards_of in cuts:
        heights = jax.random.uniform(jax.random.fold_in(jax.random.fold_in(rng, 6), axis_at), (shards_of,), jnp.float32, smallest / len(cuts), high / len(cuts))
        factor_of = factor_of * jnp.repeat(jnp.exp(heights), extent[axis_at] // shards_of).reshape((-1,) + (1,) * (len(extent) - 1 - axis_at))
    return factor_of


def gaussian(key, dims, scale, most, pieces=(), kind=jnp.bfloat16):
    result = jax.random.normal(key, dims, jnp.float32) * scale
    if len(pieces) > 0:
        result = steps_of(key, dims, pieces, -0.22, 0.18) * result
    return jnp.clip(result, min=-most, max=most).astype(kind)


def setup_inputs(seed: int = 0) -> dict:
    seeds = jax.random.split(jax.random.key(seed), 6)
    tokens = draw_tokens(jax.random.fold_in(seeds[5], 71), 0)
    in_weight = gaussian(seeds[1], (D, 2, D), D ** -0.5, 0.09375, ((2, 4),))
    short_kernel = gaussian(seeds[2], (SHORT_TAPS, 2, D), 0.6, 3.0, ((2, 4),), jnp.float32)
    long_filter = draw_long_filter(jax.random.fold_in(seeds[5], 71), 0)
    skip_gain = gaussian(seeds[4], (D,), 1.0, 4.0, ((0, 4),), jnp.float32)
    return dict(tokens=tokens, in_weight=in_weight, short_kernel=short_kernel, long_filter=long_filter, skip_gain=skip_gain)


def strand_pass(source, in_weight, short_kernel, long_filter, skip_gain):
    projected = jnp.dot(source, in_weight.reshape(D, 2 * D), preferred_element_type=jnp.float32).astype(jnp.bfloat16)
    projected = lax.optimization_barrier(projected)
    projected = projected.astype(jnp.float32).reshape(NUCLEOTIDE_COUNT, 2, D)
    summed = short_kernel[0] * projected
    for tap_index in range(1, SHORT_TAPS):
        delayed = jnp.concatenate([jnp.zeros((tap_index, 2, D), jnp.float32), projected[:-tap_index]], 0)
        summed = summed + short_kernel[tap_index] * delayed
    gate_part = summed[:, 0]
    value_part = summed[:, 1]
    length = 2 * NUCLEOTIDE_COUNT
    spectrum = jnp.fft.rfft(value_part, n=length, axis=0) * jnp.fft.rfft(long_filter, n=length, axis=0)
    convolved = jnp.fft.irfft(spectrum, n=length, axis=0)[:NUCLEOTIDE_COUNT]
    return gate_part * (convolved + skip_gain * value_part)


def reference(tokens, in_weight, short_kernel, long_filter, skip_gain):
    forward = strand_pass(tokens, in_weight, short_kernel, long_filter, skip_gain)
    reverse = strand_pass(tokens[::-1, ::-1], in_weight, short_kernel, long_filter, skip_gain)
    return (forward + reverse[::-1]).astype(jnp.bfloat16)
```

```python
import functools
import math

import jax
import jax.numpy as jnp
import numpy as np
from jax import lax
from jax.experimental import pallas as pl
from jax.experimental.pallas import tpu as pltpu
from jax.sharding import PartitionSpec as P

BF16 = jnp.bfloat16
F32 = jnp.float32
GROUP = 16
VMEM_BYTES = 56 * 1024 * 1024


def params():
    return pltpu.CompilerParams(vmem_limit_bytes=VMEM_BYTES)


def tables(blocks, rows):
    length = blocks * rows
    j1 = np.arange(blocks)
    n = np.arange(blocks)
    q = np.arange(rows)
    outer = 2 * math.pi * ((4 * j1[:, None] + 1) * n[None, :] % (4 * blocks)) / (4 * blocks)
    eye = np.eye(GROUP)
    forward = np.concatenate([np.kron(np.cos(outer), eye), np.kron(-np.sin(outer), eye)], 0)
    backward = np.concatenate([np.kron(np.cos(outer).T, eye), np.kron(-np.sin(outer).T, eye)], 1)
    turn = 2 * math.pi * ((4 * j1[:, None] + 1) * q[None, :]) / (4 * length)
    turn = np.repeat(turn, GROUP, 0)
    inner = 2 * math.pi * (q[:, None] * q[None, :] % rows) / rows
    c, s = np.cos(inner), np.sin(inner)
    inner_forward = np.block([[c, -s], [s, c]])
    inner_backward = np.block([[c, s], [-s, c]]) / length
    small = lambda a: jnp.asarray(a.astype(np.float32)).astype(BF16)
    return dict(
        forward=small(forward),
        backward=small(backward),
        turn_cos=jnp.asarray(np.cos(turn), F32),
        turn_sin=jnp.asarray(np.sin(turn), F32),
        inner_forward=small(inner_forward),
        inner_backward=small(inner_backward),
    )


def mm(a, b):
    return jnp.dot(a, b, preferred_element_type=F32)


def spectrum(x, forward, turn_cos, turn_sin, inner):
    half = forward.shape[0] // 2
    mixed = mm(forward, x)
    real, imag = mixed[:half], mixed[half:]
    turned_real = (real * turn_cos + imag * turn_sin).astype(BF16)
    turned_imag = (imag * turn_cos - real * turn_sin).astype(BF16)
    return mm(jnp.concatenate([turned_real, turned_imag], 1), inner)


def filter_prep_kernel(filter_ref, halo_ref, taps_ref, skip_ref, out_ref):
    rows, width = filter_ref.shape
    row = lax.broadcasted_iota(jnp.int32, (rows, width), 0)
    first = filter_ref[...] + jnp.where(row == 0, skip_ref[...], 0.0)
    total = taps_ref[0:1] * first
    for tap in (1, 2):
        moved = pltpu.roll(first, tap, 0)
        for edge in range(tap):
            moved = jnp.where(row == edge, halo_ref[8 - tap + edge : 9 - tap + edge], moved)
        total = total + taps_ref[tap : tap + 1] * moved
    out_ref[...] = total.T.astype(BF16)


def filter_prep(long_filter, halo, taps, skip, block=256):
    rows, width = long_filter.shape
    block = min(block, width)
    return pl.pallas_call(
        filter_prep_kernel,
        grid=(width // block,),
        in_specs=[
            pl.BlockSpec((rows, block), lambda i: (0, i)),
            pl.BlockSpec((8, block), lambda i: (0, i)),
            pl.BlockSpec((3, block), lambda i: (0, i)),
            pl.BlockSpec((1, block), lambda i: (0, i)),
        ],
        out_specs=pl.BlockSpec((block, rows), lambda i: (i, 0)),
        out_shape=jax.ShapeDtypeStruct((width, rows), BF16),
        compiler_params=params(),
        cost_estimate=pl.CostEstimate(flops=10 * rows * width, bytes_accessed=6 * rows * width, transcendentals=0),
        name="filter_prep",
    )(long_filter, halo, taps, skip)


def filter_spectrum_kernel(x_ref, forward_ref, cos_ref, sin_ref, inner_ref, out_ref):
    blocks, width, rows = x_ref.shape
    for g in range(width // GROUP):
        x = x_ref[:, g * GROUP : (g + 1) * GROUP, :].reshape(blocks * GROUP, rows)
        out_ref[g] = spectrum(x, forward_ref[...], cos_ref[...], sin_ref[...], inner_ref[...])


def filter_spectrum(x, t):
    blocks, width, rows = x.shape
    groups = width // GROUP
    return pl.pallas_call(
        filter_spectrum_kernel,
        out_shape=jax.ShapeDtypeStruct((groups, blocks * GROUP, 2 * rows), F32),
        compiler_params=params(),
        cost_estimate=pl.CostEstimate(flops=2 * 10**9, bytes_accessed=6 * 2**20, transcendentals=0),
        name="filter_spectrum",
    )(x, t["forward"], t["turn_cos"], t["turn_sin"], t["inner_forward"])


def convolve_kernel(
    x_ref, spec_ref, forward_ref, backward_ref, cos_ref, sin_ref, inner_ref, inner_back_ref, out_ref
):
    blocks, width, rows = x_ref.shape
    groups = width // GROUP
    turn_cos, turn_sin = cos_ref[...], sin_ref[...]
    for g in range(groups):
        x = x_ref[:, g * GROUP : (g + 1) * GROUP, :].reshape(blocks * GROUP, rows)
        data = spectrum(x, forward_ref[...], turn_cos, turn_sin, inner_ref[...])
        real, imag = data[:, :rows], data[:, rows:]
        filt = spec_ref.at[g % (groups // 2)]
        filter_real, filter_imag = filt[:, :rows], filt[:, rows:]
        if g >= groups // 2:
            filter_imag = -filter_imag
        prod_real = (real * filter_real - imag * filter_imag).astype(BF16)
        prod_imag = (real * filter_imag + imag * filter_real).astype(BF16)
        back = mm(jnp.concatenate([prod_real, prod_imag], 1), inner_back_ref[...])
        real, imag = back[:, :rows], back[:, rows:]
        turned_real = (real * turn_cos - imag * turn_sin).astype(BF16)
        turned_imag = (imag * turn_cos + real * turn_sin).astype(BF16)
        out = mm(backward_ref[...], jnp.concatenate([turned_real, turned_imag], 0))
        out_ref[:, g * GROUP : (g + 1) * GROUP, :] = out.astype(BF16).reshape(blocks, GROUP, rows)


def convolve(x, spec, t):
    return pl.pallas_call(
        convolve_kernel,
        out_shape=jax.ShapeDtypeStruct(x.shape, BF16),
        compiler_params=params(),
        cost_estimate=pl.CostEstimate(flops=8 * 10**9, bytes_accessed=10 * 2**20, transcendentals=0),
        name="convolve",
    )(
        x, spec, t["forward"], t["backward"], t["turn_cos"], t["turn_sin"], t["inner_forward"], t["inner_backward"]
    )


def flipped(x):
    width = x.shape[1]
    block = min(256, width)
    count = width // block
    total = lax.broadcasted_iota(jnp.int32, (block, block), 0) + lax.broadcasted_iota(jnp.int32, (block, block), 1)
    swap = jnp.where(total == block - 1, 1.0, 0.0).astype(BF16)
    parts = [mm(x[:, (count - 1 - b) * block : (count - b) * block], swap).astype(BF16) for b in range(count)]
    return jnp.concatenate(parts, 1)


def project_kernel(transposed, order_ref, own_ref, sib_ref, far_ref, farsib_ref, w_ref, out_ref, left_ref):
    rows, depth = own_ref.shape
    block = w_ref.shape[1]
    refs = (own_ref, sib_ref, far_ref, farsib_ref)

    @pl.when(pl.program_id(0) == 0)
    def _():
        for k in range(4):
            left_ref[k, :rows] = refs[k][...]
            left_ref[k, rows:] = flipped(refs[3 - k][...])

    total = jnp.zeros((2 * rows, block), F32)
    for k in range(4):
        at = pl.multiple_of(order_ref[k] * depth, depth)
        total = total + mm(left_ref[k], w_ref[pl.ds(at, depth), :])
    if transposed:
        turned = total.T.astype(BF16)
        width = out_ref.shape[1] // 2
        for d in range(out_ref.shape[0]):
            out_ref[d, :width] = turned[d * width : (d + 1) * width, :rows]
            out_ref[d, width:] = turned[d * width : (d + 1) * width, rows:]
    else:
        out_ref[...] = total.astype(BF16)


def project(order, parts, w, ctx_count, transposed, block=256):
    rows, depth = parts[0].shape
    model, width = w.shape
    block = min(block, width)
    slice_width = width // ctx_count
    if transposed:
        out_shape = (ctx_count, 2 * slice_width, rows)
        out_spec = pl.BlockSpec((block // slice_width, 2 * slice_width, rows), lambda i, o: (i, 0, 0))
    else:
        out_shape = (2 * rows, width)
        out_spec = pl.BlockSpec((2 * rows, block), lambda i, o: (0, i))
    whole = pl.BlockSpec((rows, depth), lambda i, o: (0, 0))
    return pl.pallas_call(
        functools.partial(project_kernel, transposed),
        grid_spec=pltpu.PrefetchScalarGridSpec(
            num_scalar_prefetch=1,
            grid=(width // block,),
            in_specs=[whole] * 4 + [pl.BlockSpec((model, block), lambda i, o: (0, i))],
            out_specs=out_spec,
            scratch_shapes=[pltpu.VMEM((4, 2 * rows, depth), BF16)],
        ),
        out_shape=jax.ShapeDtypeStruct(out_shape, BF16),
        compiler_params=params(),
        cost_estimate=pl.CostEstimate(
            flops=4 * rows * model * width, bytes_accessed=2 * model * width, transcendentals=0
        ),
        name="project_values" if transposed else "project_gates",
    )(order, *parts, w)


def finish_kernel(gates_ref, below_ref, above_ref, taps_ref, conv_ref, out_ref):
    rows, block = out_ref.shape
    half = conv_ref.shape[1] // 2
    row = lax.broadcasted_iota(jnp.int32, (rows, block), 0)
    forward = gates_ref[:rows].astype(F32)
    reverse = gates_ref[rows:].astype(F32)
    below = below_ref[...].astype(F32)
    above = above_ref[...].astype(F32)
    tail = below.shape[0]
    gate_forward = taps_ref[0:1] * forward
    gate_reverse = taps_ref[0:1] * reverse
    for tap in (1, 2):
        moved = pltpu.roll(forward, tap, 0)
        other = pltpu.roll(reverse, rows - tap, 0)
        for edge in range(tap):
            moved = jnp.where(row == edge, below[tail - tap + edge : tail - tap + edge + 1], moved)
            other = jnp.where(row == rows - tap + edge, above[edge : edge + 1], other)
        gate_forward = gate_forward + taps_ref[tap : tap + 1] * moved
        gate_reverse = gate_reverse + taps_ref[tap : tap + 1] * other
    conv_forward = conv_ref[:, :half].reshape(block, rows).astype(F32).T
    conv_reverse = conv_ref[:, half:].reshape(block, rows).astype(F32).T
    out_ref[...] = (gate_forward * conv_forward + gate_reverse * conv_reverse).astype(BF16)


def finish(gates, below, above, taps, conv, block=256):
    rows, width = gates.shape[0] // 2, gates.shape[1]
    block = min(block, width)
    pair = conv.shape[1]
    return pl.pallas_call(
        finish_kernel,
        grid=(width // block,),
        in_specs=[
            pl.BlockSpec((2 * rows, block), lambda i: (0, i)),
            pl.BlockSpec((below.shape[0], block), lambda i: (0, i)),
            pl.BlockSpec((above.shape[0], block), lambda i: (0, i)),
            pl.BlockSpec((3, block), lambda i: (0, i)),
            pl.BlockSpec((2 * block // pair, pair, rows), lambda i: (i, 0, 0)),
        ],
        out_specs=pl.BlockSpec((rows, block), lambda i: (0, i)),
        out_shape=jax.ShapeDtypeStruct((rows, width), BF16),
        compiler_params=params(),
        cost_estimate=pl.CostEstimate(flops=16 * rows * width, bytes_accessed=12 * rows * width, transcendentals=0),
        name="finish",
    )(gates, below, above, taps, conv)


def shards(tokens, in_weight, short_kernel, long_filter, skip_gain):
    ctx_count = lax.axis_size("ctx")
    tp_count = lax.axis_size("tp")
    ctx = lax.axis_index("ctx")
    tp = lax.axis_index("tp")
    rows, width = tokens.shape
    slice_width = width // ctx_count
    t = tables(ctx_count, rows)

    def to_tp(x, bits):
        return lax.ppermute(x, "tp", [(i, i ^ bits) for i in range(tp_count)])

    def to_next(x):
        return lax.ppermute(x, "ctx", [(i, i + 1) for i in range(ctx_count - 1)])

    def to_previous(x):
        return lax.ppermute(x, "ctx", [(i + 1, i) for i in range(ctx_count - 1)])

    def exchange(x):
        return lax.all_to_all(x, "ctx", split_axis=0, concat_axis=0, tiled=True)

    far = to_tp(tokens, 2)
    sib = to_tp(tokens, 1)
    filter_halo = to_next(long_filter[rows - 8 :])
    farsib = to_tp(far, 1)
    order = jnp.stack([tp, tp ^ 1, tp ^ 2, tp ^ 3]).astype(jnp.int32)
    parts = (tokens, sib, far, farsib)
    gate_weight = in_weight[:, 0]
    value_weight = in_weight[:, 1]
    gate_taps = short_kernel[:, 0]
    value_taps = short_kernel[:, 1]
    skip = jnp.where(ctx == 0, skip_gain, 0.0)[None, :]

    filter_rows = filter_prep(long_filter, filter_halo, value_taps, skip)
    filter_columns = exchange(filter_rows.reshape(ctx_count, slice_width, rows))
    values = project(order, parts, value_weight, ctx_count, True)
    value_columns = exchange(values)
    spec = filter_spectrum(filter_columns, t)
    conv_columns = convolve(value_columns, spec, t)
    conv = exchange(conv_columns)
    gates = project(order, parts, gate_weight, ctx_count, False)
    below = to_next(gates[rows - 16 : rows])
    above = to_previous(gates[rows : rows + 16])
    return finish(gates, below, above, gate_taps, conv)


def solution(mesh):
    placed = (P("ctx", "tp"), P(None, None, "tp"), P(None, None, "tp"), P("ctx", "tp"), P("tp"))
    return jax.shard_map(shards, mesh=mesh, in_specs=placed, out_specs=P("ctx", "tp"), check_vma=False)
```

```python
import math

import jax
import jax.numpy as jnp
import numpy as np
from jax import lax
from jax.experimental import pallas as pl
from jax.experimental.pallas import tpu as pltpu
from jax.sharding import PartitionSpec as P

BF16 = jnp.bfloat16
F32 = jnp.float32
LANES = 128
GROUP = 8
PACK = 16
MIB = 1024 * 1024
PROJECT_BYTES = 50 * MIB
CONVOLVE_BYTES = 16 * MIB
SMALL_BYTES = 10 * MIB


def params(limit):
    return pltpu.CompilerParams(vmem_limit_bytes=limit)


def cost(flops, moved):
    return pl.CostEstimate(flops=flops, bytes_accessed=moved, transcendentals=0)


def mm(a, b):
    return jnp.dot(a, b, preferred_element_type=F32)


def tables(blocks, rows):
    length = blocks * rows
    half = rows // 2
    j1 = np.arange(blocks)
    q = np.arange(rows)
    outer = 2 * math.pi * ((4 * j1[:, None] + 1) * j1[None, :] % (4 * blocks)) / (4 * blocks)
    eye = np.eye(GROUP)
    forward = np.concatenate([np.kron(np.cos(outer), eye), np.kron(-np.sin(outer), eye)], 0)
    turn = 2 * math.pi * ((4 * j1[:, None] + 1) * q[None, :]) / (4 * length)
    turn = turn[:, None, :]
    inner = []
    for odd in (0, 1):
        angle = 2 * math.pi * (q[:half, None] * (2 * q[None, :half] + odd) % rows) / rows
        c, s = np.cos(angle), np.sin(angle)
        inner.append(np.block([[c, -s], [s, c]]))
    inner = np.stack(inner)
    small = lambda a: jnp.asarray(a.astype(np.float32)).astype(BF16)
    return dict(
        forward=small(forward),
        backward=small(forward.T),
        turn_cos=jnp.asarray(np.cos(turn), F32),
        turn_sin=jnp.asarray(np.sin(turn), F32),
        inner=small(inner),
        inner_back=small(inner.transpose(0, 2, 1) / length),
    )


def turns(cos_ref, sin_ref):
    blocks, _, rows = cos_ref.shape
    wide = lambda ref: jnp.broadcast_to(ref[...], (blocks, GROUP, rows)).reshape(blocks * GROUP, rows)
    return wide(cos_ref), wide(sin_ref)


def columns_of(x_ref, pack):
    blocks, _, rows = x_ref.shape
    x = x_ref[:, pack * PACK : (pack + 1) * PACK, :].astype(F32)
    return [x[:, h * GROUP : (h + 1) * GROUP].reshape(blocks * GROUP, rows).astype(BF16) for h in range(2)]


def spectrum(x, forward, turn_cos, turn_sin, inner):
    count = x.shape[0]
    half = x.shape[1] // 2
    mixed = mm(forward, x)
    real, imag = mixed[:count], mixed[count:]
    turned_real = real * turn_cos + imag * turn_sin
    turned_imag = imag * turn_cos - real * turn_sin
    result = []
    for odd in (0, 1):
        sign = -1.0 if odd else 1.0
        parts = [(t[:, :half] + sign * t[:, half:]).astype(BF16) for t in (turned_real, turned_imag)]
        result.append(mm(jnp.concatenate(parts, 1), inner[odd]))
    return result


def filter_prep_kernel(filter_ref, out_ref):
    out_ref[...] = filter_ref[...].T.astype(BF16)


def filter_prep(long_filter, block=512):
    rows, width = long_filter.shape
    block = min(block, width)
    return pl.pallas_call(
        filter_prep_kernel,
        grid=(width // block,),
        in_specs=[pl.BlockSpec((rows, block), lambda i: (0, i))],
        out_specs=pl.BlockSpec((block, rows), lambda i: (i, 0)),
        out_shape=jax.ShapeDtypeStruct((width, rows), BF16),
        compiler_params=params(SMALL_BYTES),
        cost_estimate=cost(10 * rows * width, 6 * rows * width),
        name="filter_prep",
    )(long_filter)


def filter_spectrum(x_ref, at, taps_ref, skip_ref, forward_ref, turn_cos, turn_sin, inner_ref, out_ref):
    blocks, _, rows = x_ref.shape
    width = GROUP * out_ref.shape[0]
    local = taps_ref.shape[2]
    lane = lax.broadcasted_iota(jnp.int32, (width, local), 1)
    mine = lane - lax.broadcasted_iota(jnp.int32, (width, local), 0) == lax.axis_index("ctx") * width
    column = lambda row: jnp.sum(jnp.where(mine, row, 0.0), axis=1, keepdims=True)
    taps = [column(taps_ref[tap, 1:2]) for tap in range(3)]
    skip = column(skip_ref[...])
    position = lax.broadcasted_iota(jnp.int32, (PACK, rows), 1)
    for pack in range(width // PACK):
        these = slice(pack * PACK, (pack + 1) * PACK)
        x = x_ref[:, at + pack * PACK : at + (pack + 1) * PACK, :].astype(F32)
        first = x[:1] + jnp.where(position == 0, skip[these], 0.0)[None]
        x = jnp.concatenate([first, x[1:]], 0)
        total = taps[0][these][None] * x
        for tap in (1, 2):
            moved = pltpu.roll(x, tap, 2)
            before = jnp.concatenate([jnp.zeros((1, PACK, rows), F32), moved[:-1]], 0)
            total = total + taps[tap][these][None] * jnp.where((position < tap)[None], before, moved)
        for h in range(2):
            part = total[:, h * GROUP : (h + 1) * GROUP].reshape(blocks * GROUP, rows).astype(BF16)
            for odd, result in enumerate(spectrum(part, forward_ref[...], turn_cos, turn_sin, inner_ref)):
                out_ref[2 * pack + h, odd] = result


def convolve_kernel(
    x_ref, taps_ref, skip_ref, forward_ref, cos_ref, sin_ref, inner_ref, inner_back_ref, backward_ref, out_ref, spec_ref
):
    blocks, width, rows = out_ref.shape
    half = rows // 2
    packs = width // PACK
    turn_cos, turn_sin = turns(cos_ref, sin_ref)
    filter_spectrum(x_ref, width, taps_ref, skip_ref, forward_ref, turn_cos, turn_sin, inner_ref, spec_ref)
    for pack in range(packs):
        outs = []
        for h, x in enumerate(columns_of(x_ref, pack)):
            data = spectrum(x, forward_ref[...], turn_cos, turn_sin, inner_ref)
            back = []
            for odd in (0, 1):
                filt = spec_ref.at[2 * (pack % (packs // 2)) + h, odd]
                real, imag = data[odd][:, :half], data[odd][:, half:]
                filter_real, filter_imag = filt[:, :half], filt[:, half:]
                if pack >= packs // 2:
                    filter_imag = -filter_imag
                prod_real = (real * filter_real - imag * filter_imag).astype(BF16)
                prod_imag = (real * filter_imag + imag * filter_real).astype(BF16)
                back.append(mm(jnp.concatenate([prod_real, prod_imag], 1), inner_back_ref[odd]))
            near, far = back[0] + back[1], back[0] - back[1]
            real = jnp.concatenate([near[:, :half], far[:, :half]], 1)
            imag = jnp.concatenate([near[:, half:], far[:, half:]], 1)
            turned_real = (real * turn_cos - imag * turn_sin).astype(BF16)
            turned_imag = (imag * turn_cos + real * turn_sin).astype(BF16)
            out = mm(backward_ref[...], jnp.concatenate([turned_real, turned_imag], 0))
            outs.append(out.reshape(blocks, GROUP, rows))
        out_ref[:, pack * PACK : (pack + 1) * PACK, :] = jnp.concatenate(outs, 1).astype(BF16)


def convolve(x, taps, skip, t):
    blocks, width, rows = x.shape
    count = width // 3
    return pl.pallas_call(
        convolve_kernel,
        out_shape=jax.ShapeDtypeStruct((blocks, 2 * count, rows), BF16),
        scratch_shapes=[pltpu.VMEM((count // GROUP, 2, blocks * GROUP, rows), F32)],
        compiler_params=params(CONVOLVE_BYTES),
        cost_estimate=cost(5 * 10**9, 4 * MIB),
        name="convolve",
    )(x, taps, skip, t["forward"], t["turn_cos"], t["turn_sin"], t["inner"], t["inner_back"], t["backward"])


def swap_matrix(block):
    total = lax.broadcasted_iota(jnp.int32, (block, block), 0) + lax.broadcasted_iota(jnp.int32, (block, block), 1)
    return jnp.where(total == block - 1, 1.0, 0.0).astype(BF16)


def project_kernel(
    which, own_hbm, sib_hbm, far_hbm, farsib_hbm, w_hbm, filter_hbm, out_ref, left_ref, raw_ref, total_ref, part_sems, w_sems, filter_sem
):
    _, rows2, depth = left_ref.shape
    rows = rows2 // 2
    width = total_ref.shape[1]
    tiles = width // LANES
    block = min(256, width)
    chunk = raw_ref.shape[1]
    tp = lax.axis_index("tp")
    part_copies = [
        pltpu.make_async_copy(src, left_ref.at[k, :rows], part_sems.at[k])
        for k, src in enumerate((own_hbm, sib_hbm, far_hbm, farsib_hbm))
    ]
    w_copies = [
        pltpu.make_async_copy(
            w_hbm.at[pl.ds(pl.multiple_of((tp ^ k) * chunk, chunk), chunk)], raw_ref.at[k], w_sems.at[k]
        )
        for k in range(4)
    ]
    w_copies[0].start()
    for copy in part_copies:
        copy.start()
    for copy in w_copies[1:]:
        copy.start()
    if filter_hbm is not None:
        slice_width = filter_hbm.shape[1]
        filter_copy = pltpu.make_async_copy(filter_hbm, out_ref.at[:, 2 * slice_width :], filter_sem)
        filter_copy.start()
    for copy in part_copies:
        copy.wait()
    swap = swap_matrix(block)
    count = depth // block
    for k in range(4):
        other = left_ref[3 - k, :rows]
        for b in range(count):
            piece = mm(other[:, (count - 1 - b) * block : (count - b) * block], swap)
            left_ref[k, rows:, b * block : (b + 1) * block] = piece.astype(BF16)
    for k in range(4):
        w_copies[k].wait()
        left = left_ref[k]
        for b in range(width // block):
            cols = slice(b * block, (b + 1) * block)
            weights = [
                raw_ref[k, pl.ds(2 * tile + which, depth, stride=2 * tiles), :]
                for tile in range(b * block // LANES, (b + 1) * block // LANES)
            ]
            term = mm(left, jnp.concatenate(weights, 1))
            if k == 0:
                total_ref[:, cols] = term
            elif k < 3:
                total_ref[:, cols] += term
            else:
                total = total_ref[:, cols] + term
                if filter_hbm is not None:
                    turned = total.T.astype(BF16)
                    per = block // slice_width
                    for d in range(per):
                        part = turned[d * slice_width : (d + 1) * slice_width]
                        out_ref[b * per + d, :slice_width] = part[:, :rows]
                        out_ref[b * per + d, slice_width : 2 * slice_width] = part[:, rows:]
                else:
                    out_ref[:, cols] = total.astype(BF16)
    if filter_hbm is not None:
        filter_copy.wait()


def project(parts, weight_rows, which, width, filter_rows=None):
    rows, depth = parts[0].shape
    tiles = width // LANES
    model = weight_rows.shape[0] // (2 * tiles)
    extra = () if filter_rows is None else (filter_rows,)
    if extra:
        out_shape = (filter_rows.shape[0], 3 * filter_rows.shape[1], rows)
    else:
        out_shape = (2 * rows, width)

    def kernel(*refs):
        filter_hbm = refs[5] if extra else None
        project_kernel(which, *refs[:5], filter_hbm, *refs[5 + len(extra) :])

    return pl.pallas_call(
        kernel,
        in_specs=[pl.BlockSpec(memory_space=pl.ANY)] * (5 + len(extra)),
        out_specs=pl.BlockSpec(memory_space=pltpu.VMEM),
        scratch_shapes=[
            pltpu.VMEM((4, 2 * rows, depth), BF16),
            pltpu.VMEM((4, depth * 2 * tiles, LANES), BF16),
            pltpu.VMEM((2 * rows, width), F32),
            pltpu.SemaphoreType.DMA((4,)),
            pltpu.SemaphoreType.DMA((4,)),
            pltpu.SemaphoreType.DMA,
        ],
        out_shape=jax.ShapeDtypeStruct(out_shape, BF16),
        compiler_params=params(PROJECT_BYTES),
        cost_estimate=cost(4 * rows * model * width, 4 * model * width),
        name="project_values" if extra else "project_gates",
    )(*parts, weight_rows, *extra)


def gate_mix_kernel(gates_ref, below_ref, above_ref, taps_ref, out_ref):
    rows = gates_ref.shape[0] // 2
    block = gates_ref.shape[1]
    row = lax.broadcasted_iota(jnp.int32, (rows, block), 0)
    forward = gates_ref[:rows].astype(F32)
    reverse = gates_ref[rows:].astype(F32)
    below = below_ref[...].astype(F32)
    above = above_ref[...].astype(F32)
    tail = below.shape[0]
    gate_forward = taps_ref[0, 0:1] * forward
    gate_reverse = taps_ref[0, 0:1] * reverse
    for tap in (1, 2):
        moved = pltpu.roll(forward, tap, 0)
        other = pltpu.roll(reverse, rows - tap, 0)
        for edge in range(tap):
            moved = jnp.where(row == edge, below[tail - tap + edge : tail - tap + edge + 1], moved)
            other = jnp.where(row == rows - tap + edge, above[edge : edge + 1], other)
        gate_forward = gate_forward + taps_ref[tap, 0:1] * moved
        gate_reverse = gate_reverse + taps_ref[tap, 0:1] * other
    out_ref[0] = gate_forward.T
    out_ref[1] = gate_reverse.T


def gate_mix(gates, below, above, taps, block=256):
    rows, width = gates.shape[0] // 2, gates.shape[1]
    block = min(block, width)
    return pl.pallas_call(
        gate_mix_kernel,
        grid=(width // block,),
        in_specs=[
            pl.BlockSpec((2 * rows, block), lambda i: (0, i)),
            pl.BlockSpec((below.shape[0], block), lambda i: (0, i)),
            pl.BlockSpec((above.shape[0], block), lambda i: (0, i)),
            pl.BlockSpec((3, 2, block), lambda i: (0, 0, i)),
        ],
        out_specs=pl.BlockSpec((2, block, rows), lambda i: (0, i, 0)),
        out_shape=jax.ShapeDtypeStruct((2, width, rows), F32),
        compiler_params=params(SMALL_BYTES),
        cost_estimate=cost(16 * rows * width, 12 * rows * width),
        name="gate_mix",
    )(gates, below, above, taps)


def finish_kernel(gates_ref, conv_ref, out_ref):
    rows, block = out_ref.shape
    half = conv_ref.shape[1] // 2
    forward = conv_ref[:, :half].reshape(block, rows).astype(F32)
    reverse = conv_ref[:, half:].reshape(block, rows).astype(F32)
    out_ref[...] = (gates_ref[0] * forward + gates_ref[1] * reverse).T.astype(BF16)


def finish(gates, conv, block=256):
    _, width, rows = gates.shape
    block = min(block, width)
    pair = conv.shape[1]
    return pl.pallas_call(
        finish_kernel,
        grid=(width // block,),
        in_specs=[
            pl.BlockSpec((2, block, rows), lambda i: (0, i, 0)),
            pl.BlockSpec((2 * block // pair, pair, rows), lambda i: (i, 0, 0)),
        ],
        out_specs=pl.BlockSpec((rows, block), lambda i: (0, i)),
        out_shape=jax.ShapeDtypeStruct((rows, width), BF16),
        compiler_params=params(SMALL_BYTES),
        cost_estimate=cost(4 * rows * width, 14 * rows * width),
        name="finish",
    )(gates, conv)


def shards(tokens, in_weight, short_kernel, long_filter, skip_gain):
    ctx_count = lax.axis_size("ctx")
    tp_count = lax.axis_size("tp")
    rows, width = tokens.shape
    model = in_weight.shape[0]
    slice_width = width // ctx_count
    tiles = width // LANES
    t = tables(ctx_count, rows)

    def to_tp(x, bits):
        return lax.ppermute(x, "tp", [(i, i ^ bits) for i in range(tp_count)])

    def to_next(x):
        return lax.ppermute(x, "ctx", [(i, i + 1) for i in range(ctx_count - 1)])

    def to_previous(x):
        return lax.ppermute(x, "ctx", [(i + 1, i) for i in range(ctx_count - 1)])

    def exchange(x):
        return lax.all_to_all(x, "ctx", split_axis=0, concat_axis=0, tiled=True)

    weight_rows = in_weight.reshape(model, 2, tiles, LANES).transpose(0, 2, 1, 3).reshape(model * 2 * tiles, LANES)
    far = to_tp(tokens, 2)
    sib = to_tp(tokens, 1)
    filter_rows = filter_prep(long_filter).reshape(ctx_count, slice_width, rows)
    far, filter_rows = lax.optimization_barrier((far, filter_rows))
    farsib = to_tp(far, 1)
    parts = (tokens, sib, far, farsib)
    values = project(parts, weight_rows, 1, width, filter_rows)
    columns = exchange(values)
    parts, _ = lax.optimization_barrier((parts, values))
    gates = project(parts, weight_rows, 0, width)
    below, above = to_next(gates[rows - 16 : rows]), to_previous(gates[rows : rows + 16])
    mixed = gate_mix(gates, below, above, short_kernel)
    columns, mixed = lax.optimization_barrier((columns, mixed))
    conv = exchange(convolve(columns, short_kernel, skip_gain[None], t))
    return finish(mixed, conv)


def solution(mesh):
    placed = (P("ctx", "tp"), P(None, None, "tp"), P(None, None, "tp"), P("ctx", "tp"), P("tp"))
    return jax.shard_map(shards, mesh=mesh, in_specs=placed, out_specs=P("ctx", "tp"), check_vma=False)
```

```python
import math

import jax
import jax.numpy as jnp
import numpy as np
from jax import lax
from jax.experimental import pallas as pl
from jax.experimental.pallas import tpu as pltpu
from jax.sharding import PartitionSpec as P

BF16 = jnp.bfloat16
F32 = jnp.float32
LANES = 128
GROUP = 8
PACK = 16
MIB = 1024 * 1024
PROJECT_BYTES = 50 * MIB
START_BYTES = 36 * MIB
END_BYTES = 28 * MIB
CONVOLVE_BYTES = 16 * MIB
SMALL_BYTES = 10 * MIB


def params(limit):
    return pltpu.CompilerParams(vmem_limit_bytes=limit)


def cost(flops, moved):
    return pl.CostEstimate(flops=flops, bytes_accessed=moved, transcendentals=0)


def mm(a, b):
    return jnp.dot(a, b, preferred_element_type=F32)


def tables(blocks, rows):
    length = blocks * rows
    half = rows // 2
    j1 = np.arange(blocks)
    q = np.arange(rows)
    outer = 2 * math.pi * ((4 * j1[:, None] + 1) * j1[None, :] % (4 * blocks)) / (4 * blocks)
    eye = np.eye(GROUP)
    forward = np.concatenate([np.kron(np.cos(outer), eye), np.kron(-np.sin(outer), eye)], 0)
    turn = 2 * math.pi * ((4 * j1[:, None] + 1) * q[None, :]) / (4 * length)
    turn = turn[:, None, :]
    inner = []
    for odd in (0, 1):
        angle = 2 * math.pi * (q[:half, None] * (2 * q[None, :half] + odd) % rows) / rows
        c, s = np.cos(angle), np.sin(angle)
        inner.append(np.block([[c, -s], [s, c]]))
    inner = np.stack(inner)
    small = lambda a: jnp.asarray(a.astype(np.float32)).astype(BF16)
    return dict(
        forward=small(forward),
        backward=small(forward.T),
        turn_cos=jnp.asarray(np.cos(turn), F32),
        turn_sin=jnp.asarray(np.sin(turn), F32),
        inner=small(inner),
        inner_back=small(inner.transpose(0, 2, 1) / length),
    )


def turns(cos_ref, sin_ref):
    blocks, _, rows = cos_ref.shape
    wide = lambda ref: jnp.broadcast_to(ref[...], (blocks, GROUP, rows)).reshape(blocks * GROUP, rows)
    return wide(cos_ref), wide(sin_ref)


def columns_of(x_ref, pack):
    blocks, _, rows = x_ref.shape
    x = x_ref[:, pack * PACK : (pack + 1) * PACK, :].astype(F32)
    return [x[:, h * GROUP : (h + 1) * GROUP].reshape(blocks * GROUP, rows).astype(BF16) for h in range(2)]


def spectrum(x, forward, turn_cos, turn_sin, inner):
    count = x.shape[0]
    half = x.shape[1] // 2
    mixed = mm(forward, x)
    real, imag = mixed[:count], mixed[count:]
    turned_real = real * turn_cos + imag * turn_sin
    turned_imag = imag * turn_cos - real * turn_sin
    result = []
    for odd in (0, 1):
        sign = -1.0 if odd else 1.0
        parts = [(t[:, :half] + sign * t[:, half:]).astype(BF16) for t in (turned_real, turned_imag)]
        result.append(mm(jnp.concatenate(parts, 1), inner[odd]))
    return result


def filter_prep_kernel(filter_ref, out_ref):
    out_ref[...] = filter_ref[...].T.astype(BF16)


def filter_prep(long_filter, block=512):
    rows, width = long_filter.shape
    block = min(block, width)
    return pl.pallas_call(
        filter_prep_kernel,
        grid=(width // block,),
        in_specs=[pl.BlockSpec((rows, block), lambda i: (0, i))],
        out_specs=pl.BlockSpec((block, rows), lambda i: (i, 0)),
        out_shape=jax.ShapeDtypeStruct((width, rows), BF16),
        compiler_params=params(SMALL_BYTES),
        cost_estimate=cost(10 * rows * width, 6 * rows * width),
        name="filter_prep",
    )(long_filter)


def filter_spectrum(x_ref, at, taps_ref, skip_ref, forward_ref, turn_cos, turn_sin, inner_ref, out_ref):
    blocks, _, rows = x_ref.shape
    width = GROUP * out_ref.shape[0]
    local = taps_ref.shape[2]
    lane = lax.broadcasted_iota(jnp.int32, (width, local), 1)
    mine = lane - lax.broadcasted_iota(jnp.int32, (width, local), 0) == lax.axis_index("ctx") * width
    column = lambda row: jnp.sum(jnp.where(mine, row, 0.0), axis=1, keepdims=True)
    taps = [column(taps_ref[tap, 1:2]) for tap in range(3)]
    skip = column(skip_ref[...])
    position = lax.broadcasted_iota(jnp.int32, (PACK, rows), 1)
    for pack in range(width // PACK):
        these = slice(pack * PACK, (pack + 1) * PACK)
        x = x_ref[:, at + pack * PACK : at + (pack + 1) * PACK, :].astype(F32)
        first = x[:1] + jnp.where(position == 0, skip[these], 0.0)[None]
        x = jnp.concatenate([first, x[1:]], 0)
        total = taps[0][these][None] * x
        for tap in (1, 2):
            moved = pltpu.roll(x, tap, 2)
            before = jnp.concatenate([jnp.zeros((1, PACK, rows), F32), moved[:-1]], 0)
            total = total + taps[tap][these][None] * jnp.where((position < tap)[None], before, moved)
        for h in range(2):
            part = total[:, h * GROUP : (h + 1) * GROUP].reshape(blocks * GROUP, rows).astype(BF16)
            for odd, result in enumerate(spectrum(part, forward_ref[...], turn_cos, turn_sin, inner_ref)):
                out_ref[2 * pack + h, odd] = result


def convolve_kernel(
    x_ref, taps_ref, skip_ref, forward_ref, cos_ref, sin_ref, inner_ref, inner_back_ref, backward_ref, out_ref, spec_ref
):
    blocks, width, rows = out_ref.shape
    half = rows // 2
    packs = width // PACK
    turn_cos, turn_sin = turns(cos_ref, sin_ref)
    filter_spectrum(x_ref, width, taps_ref, skip_ref, forward_ref, turn_cos, turn_sin, inner_ref, spec_ref)
    for pack in range(packs):
        outs = []
        for h, x in enumerate(columns_of(x_ref, pack)):
            data = spectrum(x, forward_ref[...], turn_cos, turn_sin, inner_ref)
            back = []
            for odd in (0, 1):
                filt = spec_ref.at[2 * (pack % (packs // 2)) + h, odd]
                real, imag = data[odd][:, :half], data[odd][:, half:]
                filter_real, filter_imag = filt[:, :half], filt[:, half:]
                if pack >= packs // 2:
                    filter_imag = -filter_imag
                prod_real = (real * filter_real - imag * filter_imag).astype(BF16)
                prod_imag = (real * filter_imag + imag * filter_real).astype(BF16)
                back.append(mm(jnp.concatenate([prod_real, prod_imag], 1), inner_back_ref[odd]))
            near, far = back[0] + back[1], back[0] - back[1]
            real = jnp.concatenate([near[:, :half], far[:, :half]], 1)
            imag = jnp.concatenate([near[:, half:], far[:, half:]], 1)
            turned_real = (real * turn_cos - imag * turn_sin).astype(BF16)
            turned_imag = (imag * turn_cos + real * turn_sin).astype(BF16)
            out = mm(backward_ref[...], jnp.concatenate([turned_real, turned_imag], 0))
            outs.append(out.reshape(blocks, GROUP, rows))
        out_ref[:, pack * PACK : (pack + 1) * PACK, :] = jnp.concatenate(outs, 1).astype(BF16)


def convolve(x, taps, skip, t):
    blocks, width, rows = x.shape
    count = width // 3
    return pl.pallas_call(
        convolve_kernel,
        out_shape=jax.ShapeDtypeStruct((blocks, 2 * count, rows), BF16),
        scratch_shapes=[pltpu.VMEM((count // GROUP, 2, blocks * GROUP, rows), F32)],
        compiler_params=params(CONVOLVE_BYTES),
        cost_estimate=cost(5 * 10**9, 4 * MIB),
        name="convolve",
    )(x, taps, skip, t["forward"], t["turn_cos"], t["turn_sin"], t["inner"], t["inner_back"], t["backward"])


def swap_matrix(block):
    total = lax.broadcasted_iota(jnp.int32, (block, block), 0) + lax.broadcasted_iota(jnp.int32, (block, block), 1)
    return jnp.where(total == block - 1, 1.0, 0.0).astype(BF16)


def flip_into(dst, src, swap):
    block = swap.shape[0]
    count = src.shape[1] // block
    for b in range(count):
        piece = mm(src[:, (count - 1 - b) * block : (count - b) * block], swap)
        dst[:, b * block : (b + 1) * block] = piece.astype(BF16)


def picked(raw_ref, k, depth, width, first, count, which):
    tiles = width // LANES
    weights = [
        raw_ref[k, pl.ds(2 * tile + which, depth, stride=2 * tiles), :]
        for tile in range(first // LANES, (first + count) // LANES)
    ]
    return jnp.concatenate(weights, 1)


def weight_copies(w_hbm, raw_ref, sems):
    chunk = raw_ref.shape[1]
    tp = lax.axis_index("tp")
    return [
        pltpu.make_async_copy(
            w_hbm.at[pl.ds(pl.multiple_of((tp ^ k) * chunk, chunk), chunk)], raw_ref.at[k], sems.at[k]
        )
        for k in range(4)
    ]


def project_gates_kernel(
    own_hbm, sib_hbm, far_hbm, farsib_hbm, w_hbm, out_ref, left_ref, raw_ref, total_ref, part_sems, w_sems
):
    _, rows2, depth = left_ref.shape
    rows = rows2 // 2
    width = total_ref.shape[1]
    block = min(256, width)
    part_copies = [
        pltpu.make_async_copy(src, left_ref.at[k, :rows], part_sems.at[k])
        for k, src in enumerate((own_hbm, sib_hbm, far_hbm, farsib_hbm))
    ]
    w_copies = weight_copies(w_hbm, raw_ref, w_sems)
    w_copies[0].start()
    for copy in part_copies:
        copy.start()
    for copy in w_copies[1:]:
        copy.start()
    for copy in part_copies:
        copy.wait()
    swap = swap_matrix(block)
    for k in range(4):
        flip_into(left_ref.at[k, rows:], left_ref[3 - k, :rows], swap)
    for k in range(4):
        w_copies[k].wait()
        left = left_ref[k]
        for first in range(0, width, block):
            cols = slice(first, first + block)
            term = mm(left, picked(raw_ref, k, depth, width, first, block, 0))
            if k == 0:
                total_ref[:, cols] = term
            elif k < 3:
                total_ref[:, cols] += term
            else:
                out_ref[:, cols] = (total_ref[:, cols] + term).astype(BF16)


def project_gates(parts, weight_rows, width):
    rows, depth = parts[0].shape
    tiles = width // LANES
    model = weight_rows.shape[0] // (2 * tiles)
    return pl.pallas_call(
        project_gates_kernel,
        in_specs=[pl.BlockSpec(memory_space=pl.ANY)] * 5,
        out_specs=pl.BlockSpec(memory_space=pltpu.VMEM),
        scratch_shapes=[
            pltpu.VMEM((4, 2 * rows, depth), BF16),
            pltpu.VMEM((4, depth * 2 * tiles, LANES), BF16),
            pltpu.VMEM((2 * rows, width), F32),
            pltpu.SemaphoreType.DMA((4,)),
            pltpu.SemaphoreType.DMA((4,)),
        ],
        out_shape=jax.ShapeDtypeStruct((2 * rows, width), BF16),
        compiler_params=params(PROJECT_BYTES),
        cost_estimate=cost(4 * rows * model * width, 4 * model * width),
        name="project_gates",
    )(*parts, weight_rows)


def start_values_kernel(own_hbm, sib_hbm, w_hbm, total_ref, flat_hbm, left_ref, raw_ref, flat_ref, part_sems, w_sems, flat_sems):
    _, rows, depth = left_ref.shape
    width = total_ref.shape[1]
    block = min(256, width)
    part_copies = [
        pltpu.make_async_copy(src, left_ref.at[k], part_sems.at[k]) for k, src in enumerate((own_hbm, sib_hbm))
    ]
    w_copies = weight_copies(w_hbm, raw_ref, w_sems)
    flat_copies = [
        pltpu.make_async_copy(flat_ref.at[k], flat_hbm.at[k], flat_sems.at[k]) for k in range(4)
    ]
    w_copies[0].start()
    for copy in part_copies:
        copy.start()
    for copy in w_copies[1:]:
        copy.start()
    for copy in part_copies:
        copy.wait()
    swap = swap_matrix(block)
    for k in range(2):
        flip_into(left_ref.at[3 - k], left_ref[k], swap)
    for k in range(4):
        w_copies[k].wait()
        left = left_ref[k]
        here = slice(0, rows) if k < 2 else slice(rows, 2 * rows)
        for first in range(0, width, block):
            cols = slice(first, first + block)
            weights = picked(raw_ref, k, depth, width, first, block, 1)
            flat_ref[k, :, cols] = weights
            term = mm(left, weights)
            if k % 2 == 0:
                total_ref[here, cols] = term
            else:
                total_ref[here, cols] += term
        flat_copies[k].start()
    for copy in flat_copies:
        copy.wait()


def start_values(own, sib, weight_rows, width):
    rows, depth = own.shape
    tiles = width // LANES
    any_space = pl.BlockSpec(memory_space=pl.ANY)
    return pl.pallas_call(
        start_values_kernel,
        in_specs=[any_space] * 3,
        out_specs=[pl.BlockSpec(memory_space=pltpu.VMEM), any_space],
        scratch_shapes=[
            pltpu.VMEM((4, rows, depth), BF16),
            pltpu.VMEM((4, depth * 2 * tiles, LANES), BF16),
            pltpu.VMEM((4, depth, width), BF16),
            pltpu.SemaphoreType.DMA((2,)),
            pltpu.SemaphoreType.DMA((4,)),
            pltpu.SemaphoreType.DMA((4,)),
        ],
        out_shape=[
            jax.ShapeDtypeStruct((2 * rows, width), F32),
            jax.ShapeDtypeStruct((4, depth, width), BF16),
        ],
        compiler_params=params(START_BYTES),
        cost_estimate=cost(8 * rows * depth * width, 24 * depth * width),
        name="start_values",
    )(own, sib, weight_rows)


def end_values_kernel(far_ref, farsib_ref, total_ref, flat_hbm, filter_hbm, out_ref, left_ref, flat_ref, flat_sems, filter_sem):
    _, rows, depth = left_ref.shape
    width = total_ref.shape[1]
    block = min(256, width)
    slice_width = filter_hbm.shape[1]
    per = block // slice_width
    order = (2, 3, 1, 0)
    flat_copies = {
        k: pltpu.make_async_copy(flat_hbm.at[k], flat_ref.at[k], flat_sems.at[k]) for k in order
    }
    filter_copy = pltpu.make_async_copy(filter_hbm, out_ref.at[:, 2 * slice_width :], filter_sem)
    for k in order:
        flat_copies[k].start()
    filter_copy.start()
    swap = swap_matrix(block)
    flip_into(left_ref.at[0], farsib_ref[...], swap)
    flip_into(left_ref.at[1], far_ref[...], swap)
    for strand in range(2):
        here = slice(strand * rows, (strand + 1) * rows)
        one, two = (2, 3) if strand == 0 else (1, 0)
        left_one, left_two = (far_ref[...], farsib_ref[...]) if strand == 0 else (left_ref[1], left_ref[0])
        flat_copies[one].wait()
        flat_copies[two].wait()
        for b in range(width // block):
            cols = slice(b * block, (b + 1) * block)
            total = total_ref[here, cols] + mm(left_one, flat_ref[one, :, cols]) + mm(left_two, flat_ref[two, :, cols])
            turned = total.T.astype(BF16)
            for d in range(per):
                out_ref[b * per + d, strand * slice_width : (strand + 1) * slice_width] = turned[
                    d * slice_width : (d + 1) * slice_width
                ]
    filter_copy.wait()


def end_values(far, farsib, total, flat, filter_rows):
    rows, depth = far.shape
    vmem = pl.BlockSpec(memory_space=pltpu.VMEM)
    any_space = pl.BlockSpec(memory_space=pl.ANY)
    return pl.pallas_call(
        end_values_kernel,
        in_specs=[vmem] * 3 + [any_space] * 2,
        out_specs=vmem,
        scratch_shapes=[
            pltpu.VMEM((2, rows, depth), BF16),
            pltpu.VMEM(flat.shape, BF16),
            pltpu.SemaphoreType.DMA((4,)),
            pltpu.SemaphoreType.DMA,
        ],
        out_shape=jax.ShapeDtypeStruct((filter_rows.shape[0], 3 * filter_rows.shape[1], rows), BF16),
        compiler_params=params(END_BYTES),
        cost_estimate=cost(8 * rows * depth * total.shape[1], 8 * depth * total.shape[1]),
        name="end_values",
    )(far, farsib, total, flat, filter_rows)


def gate_mix_kernel(gates_ref, below_ref, above_ref, taps_ref, out_ref):
    rows = gates_ref.shape[0] // 2
    block = gates_ref.shape[1]
    row = lax.broadcasted_iota(jnp.int32, (rows, block), 0)
    forward = gates_ref[:rows].astype(F32)
    reverse = gates_ref[rows:].astype(F32)
    below = below_ref[...].astype(F32)
    above = above_ref[...].astype(F32)
    tail = below.shape[0]
    gate_forward = taps_ref[0, 0:1] * forward
    gate_reverse = taps_ref[0, 0:1] * reverse
    for tap in (1, 2):
        moved = pltpu.roll(forward, tap, 0)
        other = pltpu.roll(reverse, rows - tap, 0)
        for edge in range(tap):
            moved = jnp.where(row == edge, below[tail - tap + edge : tail - tap + edge + 1], moved)
            other = jnp.where(row == rows - tap + edge, above[edge : edge + 1], other)
        gate_forward = gate_forward + taps_ref[tap, 0:1] * moved
        gate_reverse = gate_reverse + taps_ref[tap, 0:1] * other
    out_ref[0] = gate_forward.T
    out_ref[1] = gate_reverse.T


def gate_mix(gates, below, above, taps, block=256):
    rows, width = gates.shape[0] // 2, gates.shape[1]
    block = min(block, width)
    return pl.pallas_call(
        gate_mix_kernel,
        grid=(width // block,),
        in_specs=[
            pl.BlockSpec((2 * rows, block), lambda i: (0, i)),
            pl.BlockSpec((below.shape[0], block), lambda i: (0, i)),
            pl.BlockSpec((above.shape[0], block), lambda i: (0, i)),
            pl.BlockSpec((3, 2, block), lambda i: (0, 0, i)),
        ],
        out_specs=pl.BlockSpec((2, block, rows), lambda i: (0, i, 0)),
        out_shape=jax.ShapeDtypeStruct((2, width, rows), F32),
        compiler_params=params(SMALL_BYTES),
        cost_estimate=cost(16 * rows * width, 12 * rows * width),
        name="gate_mix",
    )(gates, below, above, taps)


def finish_kernel(gates_ref, conv_ref, out_ref):
    rows, block = out_ref.shape
    half = conv_ref.shape[1] // 2
    forward = conv_ref[:, :half].reshape(block, rows).astype(F32)
    reverse = conv_ref[:, half:].reshape(block, rows).astype(F32)
    out_ref[...] = (gates_ref[0] * forward + gates_ref[1] * reverse).T.astype(BF16)


def finish(gates, conv, block=256):
    _, width, rows = gates.shape
    block = min(block, width)
    pair = conv.shape[1]
    return pl.pallas_call(
        finish_kernel,
        grid=(width // block,),
        in_specs=[
            pl.BlockSpec((2, block, rows), lambda i: (0, i, 0)),
            pl.BlockSpec((2 * block // pair, pair, rows), lambda i: (i, 0, 0)),
        ],
        out_specs=pl.BlockSpec((rows, block), lambda i: (0, i)),
        out_shape=jax.ShapeDtypeStruct((rows, width), BF16),
        compiler_params=params(SMALL_BYTES),
        cost_estimate=cost(4 * rows * width, 14 * rows * width),
        name="finish",
    )(gates, conv)


def shards(tokens, in_weight, short_kernel, long_filter, skip_gain):
    ctx_count = lax.axis_size("ctx")
    tp_count = lax.axis_size("tp")
    rows, width = tokens.shape
    model = in_weight.shape[0]
    slice_width = width // ctx_count
    tiles = width // LANES
    t = tables(ctx_count, rows)

    def to_tp(x, bits):
        return lax.ppermute(x, "tp", [(i, i ^ bits) for i in range(tp_count)])

    def to_next(x):
        return lax.ppermute(x, "ctx", [(i, i + 1) for i in range(ctx_count - 1)])

    def to_previous(x):
        return lax.ppermute(x, "ctx", [(i + 1, i) for i in range(ctx_count - 1)])

    def exchange(x):
        return lax.all_to_all(x, "ctx", split_axis=0, concat_axis=0, tiled=True)

    weight_rows = in_weight.reshape(model, 2, tiles, LANES).transpose(0, 2, 1, 3).reshape(model * 2 * tiles, LANES)
    far = to_tp(tokens, 2)
    sib = to_tp(tokens, 1)
    filter_rows = filter_prep(long_filter).reshape(ctx_count, slice_width, rows)
    total, flat = start_values(tokens, sib, weight_rows, width)
    far, filter_rows, total, flat = lax.optimization_barrier((far, filter_rows, total, flat))
    farsib = to_tp(far, 1)
    values = end_values(far, farsib, total, flat, filter_rows)
    columns = exchange(values)
    parts, _ = lax.optimization_barrier(((tokens, sib, far, farsib), values))
    gates = project_gates(parts, weight_rows, width)
    below, above = to_next(gates[rows - 16 : rows]), to_previous(gates[rows : rows + 16])
    mixed = gate_mix(gates, below, above, short_kernel)
    columns, mixed = lax.optimization_barrier((columns, mixed))
    conv = exchange(convolve(columns, short_kernel, skip_gain[None], t))
    return finish(mixed, conv)


def solution(mesh):
    placed = (P("ctx", "tp"), P(None, None, "tp"), P(None, None, "tp"), P("ctx", "tp"), P("tp"))
    return jax.shard_map(shards, mesh=mesh, in_specs=placed, out_specs=P("ctx", "tp"), check_vma=False)
```

```python
import math

import jax
import jax.numpy as jnp
import numpy as np
from jax import lax
from jax.experimental import pallas as pl
from jax.experimental.pallas import tpu as pltpu
from jax.sharding import PartitionSpec as P

BF16 = jnp.bfloat16
F32 = jnp.float32
LANES = 128
GROUP = 8
PACK = 16
MIB = 1024 * 1024
PROJECT_BYTES = 50 * MIB
START_BYTES = 36 * MIB
END_BYTES = 20 * MIB
CONVOLVE_BYTES = 16 * MIB
SMALL_BYTES = 10 * MIB


def params(limit):
    return pltpu.CompilerParams(vmem_limit_bytes=limit)


def cost(flops, moved):
    return pl.CostEstimate(flops=flops, bytes_accessed=moved, transcendentals=0)


def mm(a, b):
    return jnp.dot(a, b, preferred_element_type=F32)


def tables(blocks, rows):
    length = blocks * rows
    half = rows // 2
    j1 = np.arange(blocks)
    q = np.arange(rows)
    outer = 2 * math.pi * ((4 * j1[:, None] + 1) * j1[None, :] % (4 * blocks)) / (4 * blocks)
    eye = np.eye(GROUP)
    forward = np.concatenate([np.kron(np.cos(outer), eye), np.kron(-np.sin(outer), eye)], 0)
    turn = 2 * math.pi * ((4 * j1[:, None] + 1) * q[None, :]) / (4 * length)
    turn = turn[:, None, :]
    inner = []
    for odd in (0, 1):
        angle = 2 * math.pi * (q[:half, None] * (2 * q[None, :half] + odd) % rows) / rows
        c, s = np.cos(angle), np.sin(angle)
        inner.append(np.block([[c, -s], [s, c]]))
    inner = np.stack(inner)
    small = lambda a: jnp.asarray(a.astype(np.float32)).astype(BF16)
    return dict(
        forward=small(forward),
        backward=small(forward.T),
        turn_cos=jnp.asarray(np.cos(turn), F32),
        turn_sin=jnp.asarray(np.sin(turn), F32),
        inner=small(inner),
        inner_back=small(inner.transpose(0, 2, 1) / length),
    )


def turns(cos_ref, sin_ref):
    blocks, _, rows = cos_ref.shape
    wide = lambda ref: jnp.broadcast_to(ref[...], (blocks, GROUP, rows)).reshape(blocks * GROUP, rows)
    return wide(cos_ref), wide(sin_ref)


def columns_of(x):
    blocks, _, rows = x.shape
    return [x[:, h * GROUP : (h + 1) * GROUP].reshape(blocks * GROUP, rows).astype(BF16) for h in range(2)]


def spectrum(xs, forward, turn_cos, turn_sin, inner):
    count, rows = xs[0].shape
    half = rows // 2
    near, far = [], []
    for x in xs:
        mixed = mm(forward, x)
        real, imag = mixed[:count], mixed[count:]
        turned = (real * turn_cos + imag * turn_sin, imag * turn_cos - real * turn_sin)
        near.append(jnp.concatenate([(t[:, :half] + t[:, half:]).astype(BF16) for t in turned], 1))
        far.append(jnp.concatenate([(t[:, :half] - t[:, half:]).astype(BF16) for t in turned], 1))
    return [mm(jnp.concatenate(parts, 0), inner[odd]) for odd, parts in enumerate((near, far))]


def filter_prep_kernel(filter_ref, out_ref):
    out_ref[...] = filter_ref[...].T.astype(BF16)


def filter_prep(long_filter, block=512):
    rows, width = long_filter.shape
    block = min(block, width)
    return pl.pallas_call(
        filter_prep_kernel,
        grid=(width // block,),
        in_specs=[pl.BlockSpec((rows, block), lambda i: (0, i))],
        out_specs=pl.BlockSpec((block, rows), lambda i: (i, 0)),
        out_shape=jax.ShapeDtypeStruct((width, rows), BF16),
        compiler_params=params(SMALL_BYTES),
        cost_estimate=cost(10 * rows * width, 6 * rows * width),
        name="filter_prep",
    )(long_filter)


def filter_spectrum(x, taps, skip, forward, turn_cos, turn_sin, inner):
    rows = x.shape[2]
    position = lax.broadcasted_iota(jnp.int32, (PACK, rows), 1)
    first = x[:1] + jnp.where(position == 0, skip, 0.0)[None]
    x = jnp.concatenate([first, x[1:]], 0)
    total = taps[0][None] * x
    for tap in (1, 2):
        moved = pltpu.roll(x, tap, 2)
        before = jnp.concatenate([jnp.zeros((1, PACK, rows), F32), moved[:-1]], 0)
        total = total + taps[tap][None] * jnp.where((position < tap)[None], before, moved)
    return spectrum(columns_of(total), forward, turn_cos, turn_sin, inner)


def convolve_kernel(
    taps_ref, skip_ref, forward_ref, cos_ref, sin_ref, inner_ref, inner_back_ref, backward_ref, x_hbm,
    out_ref, x_ref, spec_ref, sems
):
    blocks, width, rows = out_ref.shape
    half = rows // 2
    count = blocks * GROUP
    packs = width // PACK
    filter_packs = spec_ref.shape[0]
    order = [packs + p for p in range(filter_packs)] + list(range(packs))
    copies = {
        p: pltpu.make_async_copy(x_hbm.at[:, p * PACK : (p + 1) * PACK], x_ref.at[p], sems.at[p]) for p in order
    }
    for p in order:
        copies[p].start()
    turn_cos, turn_sin = turns(cos_ref, sin_ref)
    local = taps_ref.shape[2]
    columns = PACK * filter_packs
    lane = lax.broadcasted_iota(jnp.int32, (columns, local), 1)
    mine = lane - lax.broadcasted_iota(jnp.int32, (columns, local), 0) == lax.axis_index("ctx") * columns
    column = lambda row: jnp.sum(jnp.where(mine, row, 0.0), axis=1, keepdims=True)
    taps = [column(taps_ref[tap, 1:2]) for tap in range(3)]
    skip = column(skip_ref[...])
    for pack in range(filter_packs):
        these = slice(pack * PACK, (pack + 1) * PACK)
        copies[packs + pack].wait()
        x = x_ref[packs + pack].astype(F32)
        result = filter_spectrum(
            x, [t[these] for t in taps], skip[these], forward_ref[...], turn_cos, turn_sin, inner_ref
        )
        for odd in (0, 1):
            spec_ref[pack, odd] = result[odd]
    for pack in range(packs):
        copies[pack].wait()
        data = spectrum(columns_of(x_ref[pack].astype(F32)), forward_ref[...], turn_cos, turn_sin, inner_ref)
        back = []
        for odd in (0, 1):
            filt = spec_ref.at[pack % filter_packs, odd]
            real, imag = data[odd][:, :half], data[odd][:, half:]
            filter_real, filter_imag = filt[:, :half], filt[:, half:]
            if pack >= filter_packs:
                filter_imag = -filter_imag
            prod_real = (real * filter_real - imag * filter_imag).astype(BF16)
            prod_imag = (real * filter_imag + imag * filter_real).astype(BF16)
            back.append(mm(jnp.concatenate([prod_real, prod_imag], 1), inner_back_ref[odd]))
        outs = []
        for h in range(2):
            even, uneven = (part[h * count : (h + 1) * count] for part in back)
            near, far = even + uneven, even - uneven
            real = jnp.concatenate([near[:, :half], far[:, :half]], 1)
            imag = jnp.concatenate([near[:, half:], far[:, half:]], 1)
            turned_real = (real * turn_cos - imag * turn_sin).astype(BF16)
            turned_imag = (imag * turn_cos + real * turn_sin).astype(BF16)
            out = mm(backward_ref[...], jnp.concatenate([turned_real, turned_imag], 0))
            outs.append(out.reshape(blocks, GROUP, rows))
        out_ref[:, pack * PACK : (pack + 1) * PACK, :] = jnp.concatenate(outs, 1).astype(BF16)


def convolve(x, taps, skip, t):
    blocks, width, rows = x.shape
    count = width // 3
    vmem = pl.BlockSpec(memory_space=pltpu.VMEM)
    return pl.pallas_call(
        convolve_kernel,
        in_specs=[vmem] * 8 + [pl.BlockSpec(memory_space=pl.ANY)],
        out_specs=vmem,
        out_shape=jax.ShapeDtypeStruct((blocks, 2 * count, rows), BF16),
        scratch_shapes=[
            pltpu.VMEM((width // PACK, blocks, PACK, rows), BF16),
            pltpu.VMEM((count // PACK, 2, 2 * blocks * GROUP, rows), F32),
            pltpu.SemaphoreType.DMA((width // PACK,)),
        ],
        compiler_params=params(CONVOLVE_BYTES),
        cost_estimate=cost(5 * 10**9, 4 * MIB),
        name="convolve",
    )(taps, skip, t["forward"], t["turn_cos"], t["turn_sin"], t["inner"], t["inner_back"], t["backward"], x)


def swap_matrix(block):
    total = lax.broadcasted_iota(jnp.int32, (block, block), 0) + lax.broadcasted_iota(jnp.int32, (block, block), 1)
    return jnp.where(total == block - 1, 1.0, 0.0).astype(BF16)


def flip_into(dst, src, swap):
    block = swap.shape[0]
    count = src.shape[1] // block
    for b in range(count):
        piece = mm(src[:, (count - 1 - b) * block : (count - b) * block], swap)
        dst[:, b * block : (b + 1) * block] = piece.astype(BF16)


def picked(raw_ref, k, depth, width, first, count, which):
    tiles = width // LANES
    weights = [
        raw_ref[k, pl.ds(2 * tile + which, depth, stride=2 * tiles), :]
        for tile in range(first // LANES, (first + count) // LANES)
    ]
    return jnp.concatenate(weights, 1)


def weight_copies(w_hbm, raw_ref, sems):
    chunk = raw_ref.shape[1]
    tp = lax.axis_index("tp")
    return [
        pltpu.make_async_copy(
            w_hbm.at[pl.ds(pl.multiple_of((tp ^ k) * chunk, chunk), chunk)], raw_ref.at[k], sems.at[k]
        )
        for k in range(4)
    ]


def project_gates_kernel(
    own_hbm, sib_hbm, far_hbm, farsib_hbm, w_hbm, out_ref, left_ref, raw_ref, total_ref, part_sems, w_sems
):
    _, rows2, depth = left_ref.shape
    rows = rows2 // 2
    width = total_ref.shape[1]
    block = min(256, width)
    part_copies = [
        pltpu.make_async_copy(src, left_ref.at[k, :rows], part_sems.at[k])
        for k, src in enumerate((own_hbm, sib_hbm, far_hbm, farsib_hbm))
    ]
    w_copies = weight_copies(w_hbm, raw_ref, w_sems)
    w_copies[0].start()
    for copy in part_copies:
        copy.start()
    for copy in w_copies[1:]:
        copy.start()
    for copy in part_copies:
        copy.wait()
    swap = swap_matrix(block)
    for k in range(4):
        flip_into(left_ref.at[k, rows:], left_ref[3 - k, :rows], swap)
    for k in range(4):
        w_copies[k].wait()
        left = left_ref[k]
        for first in range(0, width, block):
            cols = slice(first, first + block)
            term = mm(left, picked(raw_ref, k, depth, width, first, block, 0))
            if k == 0:
                total_ref[:, cols] = term
            elif k < 3:
                total_ref[:, cols] += term
            else:
                out_ref[:, cols] = (total_ref[:, cols] + term).astype(BF16)


def project_gates(parts, weight_rows, width):
    rows, depth = parts[0].shape
    tiles = width // LANES
    model = weight_rows.shape[0] // (2 * tiles)
    return pl.pallas_call(
        project_gates_kernel,
        in_specs=[pl.BlockSpec(memory_space=pl.ANY)] * 5,
        out_specs=pl.BlockSpec(memory_space=pltpu.VMEM),
        scratch_shapes=[
            pltpu.VMEM((4, 2 * rows, depth), BF16),
            pltpu.VMEM((4, depth * 2 * tiles, LANES), BF16),
            pltpu.VMEM((2 * rows, width), F32),
            pltpu.SemaphoreType.DMA((4,)),
            pltpu.SemaphoreType.DMA((4,)),
        ],
        out_shape=jax.ShapeDtypeStruct((2 * rows, width), BF16),
        compiler_params=params(PROJECT_BYTES),
        cost_estimate=cost(4 * rows * model * width, 4 * model * width),
        name="project_gates",
    )(*parts, weight_rows)


def start_values_kernel(own_hbm, sib_hbm, w_hbm, total_ref, flat_hbm, left_ref, raw_ref, flat_ref, part_sems, w_sems, flat_sems):
    _, rows, depth = left_ref.shape
    width = total_ref.shape[1]
    block = min(256, width)
    part_copies = [
        pltpu.make_async_copy(src, left_ref.at[k], part_sems.at[k]) for k, src in enumerate((own_hbm, sib_hbm))
    ]
    w_copies = weight_copies(w_hbm, raw_ref, w_sems)
    flat_copies = [
        pltpu.make_async_copy(flat_ref.at[k], flat_hbm.at[k], flat_sems.at[k]) for k in range(4)
    ]
    w_copies[0].start()
    for copy in part_copies:
        copy.start()
    for copy in w_copies[1:]:
        copy.start()
    for copy in part_copies:
        copy.wait()
    swap = swap_matrix(block)
    for k in range(2):
        flip_into(left_ref.at[3 - k], left_ref[k], swap)
    for k in range(4):
        w_copies[k].wait()
        left = left_ref[k]
        here = slice(0, rows) if k < 2 else slice(rows, 2 * rows)
        for first in range(0, width, block):
            cols = slice(first, first + block)
            weights = picked(raw_ref, k, depth, width, first, block, 1)
            flat_ref[k, :, cols] = weights
            term = mm(left, weights)
            if k % 2 == 0:
                total_ref[here, cols] = term
            else:
                total_ref[here, cols] += term
        flat_copies[k].start()
    for copy in flat_copies:
        copy.wait()


def start_values(own, sib, weight_rows, width):
    rows, depth = own.shape
    tiles = width // LANES
    any_space = pl.BlockSpec(memory_space=pl.ANY)
    return pl.pallas_call(
        start_values_kernel,
        in_specs=[any_space] * 3,
        out_specs=[pl.BlockSpec(memory_space=pltpu.VMEM), any_space],
        scratch_shapes=[
            pltpu.VMEM((4, rows, depth), BF16),
            pltpu.VMEM((4, depth * 2 * tiles, LANES), BF16),
            pltpu.VMEM((4, depth, width), BF16),
            pltpu.SemaphoreType.DMA((2,)),
            pltpu.SemaphoreType.DMA((4,)),
            pltpu.SemaphoreType.DMA((4,)),
        ],
        out_shape=[
            jax.ShapeDtypeStruct((2 * rows, width), F32),
            jax.ShapeDtypeStruct((4, depth, width), BF16),
        ],
        compiler_params=params(START_BYTES),
        cost_estimate=cost(8 * rows * depth * width, 24 * depth * width),
        name="start_values",
    )(own, sib, weight_rows)


def add_values_kernel(last, part_ref, total_ref, flat_hbm, *refs):
    if last:
        filter_hbm, out_ref, left_ref, flat_ref, flat_sems, filter_sem = refs
        slice_width = filter_hbm.shape[1]
        filter_copy = pltpu.make_async_copy(filter_hbm, out_ref.at[:, 2 * slice_width :], filter_sem)
    else:
        out_ref, left_ref, flat_ref, flat_sems = refs
    rows, depth = left_ref.shape
    width = total_ref.shape[1]
    block = min(256, width)
    chunks = (3, 0) if last else (2, 1)
    copies = [
        pltpu.make_async_copy(flat_hbm.at[k], flat_ref.at[strand], flat_sems.at[strand])
        for strand, k in enumerate(chunks)
    ]
    for copy in copies:
        copy.start()
    if last:
        filter_copy.start()
    flip_into(left_ref, part_ref[...], swap_matrix(block))
    for strand in range(2):
        here = slice(strand * rows, (strand + 1) * rows)
        left = part_ref[...] if strand == 0 else left_ref[...]
        copies[strand].wait()
        for b in range(width // block):
            cols = slice(b * block, (b + 1) * block)
            total = total_ref[here, cols] + mm(left, flat_ref[strand, :, cols])
            if last:
                turned = total.T.astype(BF16)
                per = block // slice_width
                for d in range(per):
                    out_ref[b * per + d, strand * slice_width : (strand + 1) * slice_width] = turned[
                        d * slice_width : (d + 1) * slice_width
                    ]
            else:
                out_ref[here, cols] = total
    if last:
        filter_copy.wait()


def add_values(part, total, flat, filter_rows=None):
    rows, depth = part.shape
    width = total.shape[1]
    vmem = pl.BlockSpec(memory_space=pltpu.VMEM)
    any_space = pl.BlockSpec(memory_space=pl.ANY)
    last = filter_rows is not None
    extra = (filter_rows,) if last else ()
    if last:
        out_shape = jax.ShapeDtypeStruct((filter_rows.shape[0], 3 * filter_rows.shape[1], rows), BF16)
    else:
        out_shape = jax.ShapeDtypeStruct(total.shape, F32)

    def kernel(*refs):
        add_values_kernel(last, *refs)

    return pl.pallas_call(
        kernel,
        in_specs=[vmem] * 2 + [any_space] * (1 + len(extra)),
        out_specs=vmem,
        scratch_shapes=[
            pltpu.VMEM((rows, depth), BF16),
            pltpu.VMEM((2, depth, width), BF16),
            pltpu.SemaphoreType.DMA((2,)),
        ]
        + [pltpu.SemaphoreType.DMA] * len(extra),
        out_shape=out_shape,
        compiler_params=params(END_BYTES),
        cost_estimate=cost(4 * rows * depth * width, 4 * depth * width),
        name="last_values" if last else "far_values",
    )(part, total, flat, *extra)


def gate_mix_kernel(gates_ref, below_ref, above_ref, taps_ref, out_ref):
    rows = gates_ref.shape[0] // 2
    block = gates_ref.shape[1]
    row = lax.broadcasted_iota(jnp.int32, (rows, block), 0)
    forward = gates_ref[:rows].astype(F32)
    reverse = gates_ref[rows:].astype(F32)
    below = below_ref[...].astype(F32)
    above = above_ref[...].astype(F32)
    tail = below.shape[0]
    gate_forward = taps_ref[0, 0:1] * forward
    gate_reverse = taps_ref[0, 0:1] * reverse
    for tap in (1, 2):
        moved = pltpu.roll(forward, tap, 0)
        other = pltpu.roll(reverse, rows - tap, 0)
        for edge in range(tap):
            moved = jnp.where(row == edge, below[tail - tap + edge : tail - tap + edge + 1], moved)
            other = jnp.where(row == rows - tap + edge, above[edge : edge + 1], other)
        gate_forward = gate_forward + taps_ref[tap, 0:1] * moved
        gate_reverse = gate_reverse + taps_ref[tap, 0:1] * other
    out_ref[0] = gate_forward.T
    out_ref[1] = gate_reverse.T


def gate_mix(gates, below, above, taps, block=256):
    rows, width = gates.shape[0] // 2, gates.shape[1]
    block = min(block, width)
    return pl.pallas_call(
        gate_mix_kernel,
        grid=(width // block,),
        in_specs=[
            pl.BlockSpec((2 * rows, block), lambda i: (0, i)),
            pl.BlockSpec((below.shape[0], block), lambda i: (0, i)),
            pl.BlockSpec((above.shape[0], block), lambda i: (0, i)),
            pl.BlockSpec((3, 2, block), lambda i: (0, 0, i)),
        ],
        out_specs=pl.BlockSpec((2, block, rows), lambda i: (0, i, 0)),
        out_shape=jax.ShapeDtypeStruct((2, width, rows), F32),
        compiler_params=params(SMALL_BYTES),
        cost_estimate=cost(16 * rows * width, 12 * rows * width),
        name="gate_mix",
    )(gates, below, above, taps)


def finish_kernel(gates_ref, conv_ref, out_ref):
    rows, block = out_ref.shape
    half = conv_ref.shape[1] // 2
    forward = conv_ref[:, :half].reshape(block, rows).astype(F32)
    reverse = conv_ref[:, half:].reshape(block, rows).astype(F32)
    out_ref[...] = (gates_ref[0] * forward + gates_ref[1] * reverse).T.astype(BF16)


def finish(gates, conv, block=256):
    _, width, rows = gates.shape
    block = min(block, width)
    pair = conv.shape[1]
    return pl.pallas_call(
        finish_kernel,
        grid=(width // block,),
        in_specs=[
            pl.BlockSpec((2, block, rows), lambda i: (0, i, 0)),
            pl.BlockSpec((2 * block // pair, pair, rows), lambda i: (i, 0, 0)),
        ],
        out_specs=pl.BlockSpec((rows, block), lambda i: (0, i)),
        out_shape=jax.ShapeDtypeStruct((rows, width), BF16),
        compiler_params=params(SMALL_BYTES),
        cost_estimate=cost(4 * rows * width, 14 * rows * width),
        name="finish",
    )(gates, conv)


def shards(tokens, in_weight, short_kernel, long_filter, skip_gain):
    ctx_count = lax.axis_size("ctx")
    tp_count = lax.axis_size("tp")
    rows, width = tokens.shape
    model = in_weight.shape[0]
    slice_width = width // ctx_count
    tiles = width // LANES
    t = tables(ctx_count, rows)

    def to_tp(x, bits):
        return lax.ppermute(x, "tp", [(i, i ^ bits) for i in range(tp_count)])

    def to_next(x):
        return lax.ppermute(x, "ctx", [(i, i + 1) for i in range(ctx_count - 1)])

    def to_previous(x):
        return lax.ppermute(x, "ctx", [(i + 1, i) for i in range(ctx_count - 1)])

    def exchange(x):
        return lax.all_to_all(x, "ctx", split_axis=0, concat_axis=0, tiled=True)

    weight_rows = in_weight.reshape(model, 2, tiles, LANES).transpose(0, 2, 1, 3).reshape(model * 2 * tiles, LANES)
    far = to_tp(tokens, 2)
    sib = to_tp(tokens, 1)
    filter_rows = filter_prep(long_filter).reshape(ctx_count, slice_width, rows)
    total, flat = start_values(tokens, sib, weight_rows, width)
    far, filter_rows, total, flat = lax.optimization_barrier((far, filter_rows, total, flat))
    farsib = to_tp(far, 1)
    total = add_values(far, total, flat)
    values = add_values(farsib, total, flat, filter_rows)
    columns = exchange(values)
    parts, _ = lax.optimization_barrier(((tokens, sib, far, farsib), values))
    gates = project_gates(parts, weight_rows, width)
    below, above = to_next(gates[rows - 16 : rows]), to_previous(gates[rows : rows + 16])
    mixed = gate_mix(gates, below, above, short_kernel)
    columns, mixed = lax.optimization_barrier((columns, mixed))
    conv = exchange(convolve(columns, short_kernel, skip_gain[None], t))
    return finish(mixed, conv)


def solution(mesh):
    placed = (P("ctx", "tp"), P(None, None, "tp"), P(None, None, "tp"), P("ctx", "tp"), P("tp"))
    return jax.shard_map(shards, mesh=mesh, in_specs=placed, out_specs=P("ctx", "tp"), check_vma=False)
```

```python
import math

import jax
import jax.numpy as jnp
import numpy as np
from jax import lax
from jax.experimental import pallas as pl
from jax.experimental.pallas import tpu as pltpu
from jax.sharding import PartitionSpec as P

BF16 = jnp.bfloat16
F32 = jnp.float32
LANES = 128
GROUP = 8
PACK = 16
MIB = 1024 * 1024
PROJECT_BYTES = 50 * MIB
START_BYTES = 36 * MIB
END_BYTES = 20 * MIB
CONVOLVE_BYTES = 16 * MIB
SMALL_BYTES = 10 * MIB


def params(limit):
    return pltpu.CompilerParams(vmem_limit_bytes=limit)


def cost(flops, moved):
    return pl.CostEstimate(flops=flops, bytes_accessed=moved, transcendentals=0)


def mm(a, b):
    return jnp.dot(a, b, preferred_element_type=F32)


def tables(blocks, rows):
    length = blocks * rows
    half = rows // 2
    j1 = np.arange(blocks)
    q = np.arange(rows)
    outer = 2 * math.pi * ((4 * j1[:, None] + 1) * j1[None, :] % (4 * blocks)) / (4 * blocks)
    eye = np.eye(GROUP)
    forward = np.concatenate([np.kron(np.cos(outer), eye), np.kron(-np.sin(outer), eye)], 0)
    turn = 2 * math.pi * ((4 * j1[:, None] + 1) * q[None, :]) / (4 * length)
    turn = turn[:, None, :]
    inner = []
    for odd in (0, 1):
        angle = 2 * math.pi * (q[:half, None] * (2 * q[None, :half] + odd) % rows) / rows
        c, s = np.cos(angle), np.sin(angle)
        inner.append(np.block([[c, -s], [s, c]]))
    inner = np.stack(inner)
    small = lambda a: jnp.asarray(a.astype(np.float32)).astype(BF16)
    return dict(
        forward=small(forward),
        backward=small(forward.T),
        turn_cos=jnp.asarray(np.cos(turn), F32),
        turn_sin=jnp.asarray(np.sin(turn), F32),
        inner=small(inner),
        inner_back=small(inner.transpose(0, 2, 1) / length),
    )


def turns(cos_ref, sin_ref):
    blocks, _, rows = cos_ref.shape
    wide = lambda ref: jnp.broadcast_to(ref[...], (blocks, GROUP, rows)).reshape(blocks * GROUP, rows)
    return wide(cos_ref), wide(sin_ref)


def columns_of(x):
    blocks, _, rows = x.shape
    return [x[:, h * GROUP : (h + 1) * GROUP].reshape(blocks * GROUP, rows).astype(BF16) for h in range(2)]


def spectrum(xs, forward, turn_cos, turn_sin, inner):
    count, rows = xs[0].shape
    half = rows // 2
    near, far = [], []
    for x in xs:
        mixed = mm(forward, x)
        real, imag = mixed[:count], mixed[count:]
        turned = (real * turn_cos + imag * turn_sin, imag * turn_cos - real * turn_sin)
        near.append(jnp.concatenate([(t[:, :half] + t[:, half:]).astype(BF16) for t in turned], 1))
        far.append(jnp.concatenate([(t[:, :half] - t[:, half:]).astype(BF16) for t in turned], 1))
    return [mm(jnp.concatenate(parts, 0), inner[odd]) for odd, parts in enumerate((near, far))]


def filter_prep_kernel(filter_ref, out_ref):
    out_ref[...] = filter_ref[...].T.astype(BF16)


def filter_prep(long_filter, block=512):
    rows, width = long_filter.shape
    block = min(block, width)
    return pl.pallas_call(
        filter_prep_kernel,
        grid=(width // block,),
        in_specs=[pl.BlockSpec((rows, block), lambda i: (0, i))],
        out_specs=pl.BlockSpec((block, rows), lambda i: (i, 0)),
        out_shape=jax.ShapeDtypeStruct((width, rows), BF16),
        compiler_params=params(SMALL_BYTES),
        cost_estimate=cost(10 * rows * width, 6 * rows * width),
        name="filter_prep",
    )(long_filter)


def filter_spectrum(x, taps, skip, forward, turn_cos, turn_sin, inner):
    rows = x.shape[2]
    position = lax.broadcasted_iota(jnp.int32, (PACK, rows), 1)
    first = x[:1] + jnp.where(position == 0, skip, 0.0)[None]
    x = jnp.concatenate([first, x[1:]], 0)
    total = taps[0][None] * x
    for tap in (1, 2):
        moved = pltpu.roll(x, tap, 2)
        before = jnp.concatenate([jnp.zeros((1, PACK, rows), F32), moved[:-1]], 0)
        total = total + taps[tap][None] * jnp.where((position < tap)[None], before, moved)
    return spectrum(columns_of(total), forward, turn_cos, turn_sin, inner)


def convolve_kernel(
    taps_ref, skip_ref, forward_ref, cos_ref, sin_ref, inner_ref, inner_back_ref, backward_ref, x_hbm,
    out_ref, x_ref, spec_ref, sems
):
    blocks, width, rows = out_ref.shape
    half = rows // 2
    count = blocks * GROUP
    packs = width // PACK
    filter_packs = spec_ref.shape[0]
    order = [packs + p for p in range(filter_packs)] + list(range(packs))
    copies = {
        p: pltpu.make_async_copy(x_hbm.at[:, p * PACK : (p + 1) * PACK], x_ref.at[p], sems.at[p]) for p in order
    }
    for p in order:
        copies[p].start()
    turn_cos, turn_sin = turns(cos_ref, sin_ref)
    local = taps_ref.shape[2]
    columns = PACK * filter_packs
    lane = lax.broadcasted_iota(jnp.int32, (columns, local), 1)
    mine = lane - lax.broadcasted_iota(jnp.int32, (columns, local), 0) == lax.axis_index("ctx") * columns
    column = lambda row: jnp.sum(jnp.where(mine, row, 0.0), axis=1, keepdims=True)
    taps = [column(taps_ref[tap, 1:2]) for tap in range(3)]
    skip = column(skip_ref[...])
    for pack in range(filter_packs):
        these = slice(pack * PACK, (pack + 1) * PACK)
        copies[packs + pack].wait()
        x = x_ref[packs + pack].astype(F32)
        result = filter_spectrum(
            x, [t[these] for t in taps], skip[these], forward_ref[...], turn_cos, turn_sin, inner_ref
        )
        for odd in (0, 1):
            spec_ref[pack, odd] = result[odd]
    for pack in range(packs):
        copies[pack].wait()
        data = spectrum(columns_of(x_ref[pack].astype(F32)), forward_ref[...], turn_cos, turn_sin, inner_ref)
        back = []
        for odd in (0, 1):
            filt = spec_ref.at[pack % filter_packs, odd]
            real, imag = data[odd][:, :half], data[odd][:, half:]
            filter_real, filter_imag = filt[:, :half], filt[:, half:]
            if pack >= filter_packs:
                filter_imag = -filter_imag
            prod_real = (real * filter_real - imag * filter_imag).astype(BF16)
            prod_imag = (real * filter_imag + imag * filter_real).astype(BF16)
            back.append(mm(jnp.concatenate([prod_real, prod_imag], 1), inner_back_ref[odd]))
        outs = []
        for h in range(2):
            even, uneven = (part[h * count : (h + 1) * count] for part in back)
            near, far = even + uneven, even - uneven
            real = jnp.concatenate([near[:, :half], far[:, :half]], 1)
            imag = jnp.concatenate([near[:, half:], far[:, half:]], 1)
            turned_real = (real * turn_cos - imag * turn_sin).astype(BF16)
            turned_imag = (imag * turn_cos + real * turn_sin).astype(BF16)
            out = mm(backward_ref[...], jnp.concatenate([turned_real, turned_imag], 0))
            outs.append(out.reshape(blocks, GROUP, rows))
        out_ref[:, pack * PACK : (pack + 1) * PACK, :] = jnp.concatenate(outs, 1).astype(BF16)


def convolve(x, taps, skip, t):
    blocks, width, rows = x.shape
    count = width // 3
    vmem = pl.BlockSpec(memory_space=pltpu.VMEM)
    return pl.pallas_call(
        convolve_kernel,
        in_specs=[vmem] * 8 + [pl.BlockSpec(memory_space=pl.ANY)],
        out_specs=vmem,
        out_shape=jax.ShapeDtypeStruct((blocks, 2 * count, rows), BF16),
        scratch_shapes=[
            pltpu.VMEM((width // PACK, blocks, PACK, rows), BF16),
            pltpu.VMEM((count // PACK, 2, 2 * blocks * GROUP, rows), F32),
            pltpu.SemaphoreType.DMA((width // PACK,)),
        ],
        compiler_params=params(CONVOLVE_BYTES),
        cost_estimate=cost(5 * 10**9, 4 * MIB),
        name="convolve",
    )(taps, skip, t["forward"], t["turn_cos"], t["turn_sin"], t["inner"], t["inner_back"], t["backward"], x)


def swap_matrix(block):
    total = lax.broadcasted_iota(jnp.int32, (block, block), 0) + lax.broadcasted_iota(jnp.int32, (block, block), 1)
    return jnp.where(total == block - 1, 1.0, 0.0).astype(BF16)


def flip_into(dst, src, swap):
    block = swap.shape[0]
    count = src.shape[1] // block
    for b in range(count):
        piece = mm(src[:, (count - 1 - b) * block : (count - b) * block], swap)
        dst[:, b * block : (b + 1) * block] = piece.astype(BF16)


def picked(raw_ref, k, depth, width, first, count, which):
    tiles = width // LANES
    weights = [
        raw_ref[k, pl.ds(2 * tile + which, depth, stride=2 * tiles), :]
        for tile in range(first // LANES, (first + count) // LANES)
    ]
    return jnp.concatenate(weights, 1)


def weight_copies(w_hbm, raw_ref, sems):
    chunk = raw_ref.shape[1]
    tp = lax.axis_index("tp")
    return [
        pltpu.make_async_copy(
            w_hbm.at[pl.ds(pl.multiple_of((tp ^ k) * chunk, chunk), chunk)], raw_ref.at[k], sems.at[k]
        )
        for k in range(4)
    ]


def project_gates_kernel(
    own_hbm, sib_hbm, far_hbm, farsib_hbm, w_hbm, out_ref, left_ref, raw_ref, total_ref, part_sems, w_sems
):
    _, rows2, depth = left_ref.shape
    rows = rows2 // 2
    width = total_ref.shape[1]
    block = min(256, width)
    part_copies = [
        pltpu.make_async_copy(src, left_ref.at[k, :rows], part_sems.at[k])
        for k, src in enumerate((own_hbm, sib_hbm, far_hbm, farsib_hbm))
    ]
    w_copies = weight_copies(w_hbm, raw_ref, w_sems)
    w_copies[0].start()
    for copy in part_copies:
        copy.start()
    for copy in w_copies[1:]:
        copy.start()
    for copy in part_copies:
        copy.wait()
    swap = swap_matrix(block)
    for k in range(4):
        flip_into(left_ref.at[k, rows:], left_ref[3 - k, :rows], swap)
    for k in range(4):
        w_copies[k].wait()
        left = left_ref[k]
        for first in range(0, width, block):
            cols = slice(first, first + block)
            term = mm(left, picked(raw_ref, k, depth, width, first, block, 0))
            if k == 0:
                total_ref[:, cols] = term
            elif k < 3:
                total_ref[:, cols] += term
            else:
                out_ref[:, cols] = (total_ref[:, cols] + term).astype(BF16)


def project_gates(parts, weight_rows, width):
    rows, depth = parts[0].shape
    tiles = width // LANES
    model = weight_rows.shape[0] // (2 * tiles)
    return pl.pallas_call(
        project_gates_kernel,
        in_specs=[pl.BlockSpec(memory_space=pl.ANY)] * 5,
        out_specs=pl.BlockSpec(memory_space=pltpu.VMEM),
        scratch_shapes=[
            pltpu.VMEM((4, 2 * rows, depth), BF16),
            pltpu.VMEM((4, depth * 2 * tiles, LANES), BF16),
            pltpu.VMEM((2 * rows, width), F32),
            pltpu.SemaphoreType.DMA((4,)),
            pltpu.SemaphoreType.DMA((4,)),
        ],
        out_shape=jax.ShapeDtypeStruct((2 * rows, width), BF16),
        compiler_params=params(PROJECT_BYTES),
        cost_estimate=cost(4 * rows * model * width, 4 * model * width),
        name="project_gates",
    )(*parts, weight_rows)


def start_values_kernel(
    own_hbm, sib_hbm, w_hbm, total_ref, flat_far_hbm, flat_last_hbm, left_ref, raw_ref, flat_ref, part_sems, w_sems, flat_sems
):
    _, rows, depth = left_ref.shape
    width = total_ref.shape[1]
    block = min(256, width)
    part_copies = [
        pltpu.make_async_copy(src, left_ref.at[k], part_sems.at[k]) for k, src in enumerate((own_hbm, sib_hbm))
    ]
    w_copies = weight_copies(w_hbm, raw_ref, w_sems)
    flat_copies = [
        pltpu.make_async_copy(flat_ref.at[k], dst, flat_sems.at[k])
        for k, dst in enumerate((flat_last_hbm.at[1], flat_far_hbm.at[1], flat_far_hbm.at[0], flat_last_hbm.at[0]))
    ]
    w_copies[0].start()
    for copy in part_copies:
        copy.start()
    for copy in w_copies[1:]:
        copy.start()
    for copy in part_copies:
        copy.wait()
    swap = swap_matrix(block)
    for k in range(2):
        flip_into(left_ref.at[3 - k], left_ref[k], swap)
    for k in range(4):
        w_copies[k].wait()
        left = left_ref[k]
        here = slice(0, rows) if k < 2 else slice(rows, 2 * rows)
        for first in range(0, width, block):
            cols = slice(first, first + block)
            weights = picked(raw_ref, k, depth, width, first, block, 1)
            flat_ref[k, :, cols] = weights
            term = mm(left, weights)
            if k % 2 == 0:
                total_ref[here, cols] = term
            else:
                total_ref[here, cols] += term
        flat_copies[k].start()
    for copy in flat_copies:
        copy.wait()


def start_values(own, sib, weight_rows, width):
    rows, depth = own.shape
    tiles = width // LANES
    any_space = pl.BlockSpec(memory_space=pl.ANY)
    return pl.pallas_call(
        start_values_kernel,
        in_specs=[any_space] * 3,
        out_specs=[pl.BlockSpec(memory_space=pltpu.VMEM), any_space, any_space],
        scratch_shapes=[
            pltpu.VMEM((4, rows, depth), BF16),
            pltpu.VMEM((4, depth * 2 * tiles, LANES), BF16),
            pltpu.VMEM((4, depth, width), BF16),
            pltpu.SemaphoreType.DMA((2,)),
            pltpu.SemaphoreType.DMA((4,)),
            pltpu.SemaphoreType.DMA((4,)),
        ],
        out_shape=[
            jax.ShapeDtypeStruct((2 * rows, width), F32),
            jax.ShapeDtypeStruct((2, depth, width), BF16),
            jax.ShapeDtypeStruct((2, depth, width), BF16),
        ],
        compiler_params=params(START_BYTES),
        cost_estimate=cost(8 * rows * depth * width, 24 * depth * width),
        name="start_values",
    )(own, sib, weight_rows)


def add_values_kernel(last, part_ref, total_ref, flat_ref, *refs):
    if last:
        filter_hbm, out_ref, left_ref, filter_sem = refs
        slice_width = filter_hbm.shape[1]
        filter_copy = pltpu.make_async_copy(filter_hbm, out_ref.at[:, 2 * slice_width :], filter_sem)
    else:
        out_ref, left_ref = refs
    rows, depth = left_ref.shape
    width = total_ref.shape[1]
    block = min(256, width)
    if last:
        filter_copy.start()
    flip_into(left_ref, part_ref[...], swap_matrix(block))
    for strand in range(2):
        here = slice(strand * rows, (strand + 1) * rows)
        left = part_ref[...] if strand == 0 else left_ref[...]
        for b in range(width // block):
            cols = slice(b * block, (b + 1) * block)
            total = total_ref[here, cols] + mm(left, flat_ref[strand, :, cols])
            if last:
                turned = total.T.astype(BF16)
                per = block // slice_width
                for d in range(per):
                    out_ref[b * per + d, strand * slice_width : (strand + 1) * slice_width] = turned[
                        d * slice_width : (d + 1) * slice_width
                    ]
            else:
                out_ref[here, cols] = total
    if last:
        filter_copy.wait()


def add_values(part, total, flat, filter_rows=None):
    rows, depth = part.shape
    width = total.shape[1]
    vmem = pl.BlockSpec(memory_space=pltpu.VMEM)
    any_space = pl.BlockSpec(memory_space=pl.ANY)
    last = filter_rows is not None
    extra = (filter_rows,) if last else ()
    if last:
        out_shape = jax.ShapeDtypeStruct((filter_rows.shape[0], 3 * filter_rows.shape[1], rows), BF16)
    else:
        out_shape = jax.ShapeDtypeStruct(total.shape, F32)

    def kernel(*refs):
        add_values_kernel(last, *refs)

    return pl.pallas_call(
        kernel,
        in_specs=[vmem] * 3 + [any_space] * len(extra),
        out_specs=vmem,
        scratch_shapes=[pltpu.VMEM((rows, depth), BF16)] + [pltpu.SemaphoreType.DMA] * len(extra),
        out_shape=out_shape,
        compiler_params=params(END_BYTES),
        cost_estimate=cost(4 * rows * depth * width, 4 * depth * width),
        name="last_values" if last else "far_values",
    )(part, total, flat, *extra)


def gate_mix_kernel(gates_ref, below_ref, above_ref, taps_ref, out_ref):
    rows = gates_ref.shape[0] // 2
    block = gates_ref.shape[1]
    row = lax.broadcasted_iota(jnp.int32, (rows, block), 0)
    forward = gates_ref[:rows].astype(F32)
    reverse = gates_ref[rows:].astype(F32)
    below = below_ref[...].astype(F32)
    above = above_ref[...].astype(F32)
    tail = below.shape[0]
    gate_forward = taps_ref[0, 0:1] * forward
    gate_reverse = taps_ref[0, 0:1] * reverse
    for tap in (1, 2):
        moved = pltpu.roll(forward, tap, 0)
        other = pltpu.roll(reverse, rows - tap, 0)
        for edge in range(tap):
            moved = jnp.where(row == edge, below[tail - tap + edge : tail - tap + edge + 1], moved)
            other = jnp.where(row == rows - tap + edge, above[edge : edge + 1], other)
        gate_forward = gate_forward + taps_ref[tap, 0:1] * moved
        gate_reverse = gate_reverse + taps_ref[tap, 0:1] * other
    out_ref[0] = gate_forward.T
    out_ref[1] = gate_reverse.T


def gate_mix(gates, below, above, taps, block=256):
    rows, width = gates.shape[0] // 2, gates.shape[1]
    block = min(block, width)
    return pl.pallas_call(
        gate_mix_kernel,
        grid=(width // block,),
        in_specs=[
            pl.BlockSpec((2 * rows, block), lambda i: (0, i)),
            pl.BlockSpec((below.shape[0], block), lambda i: (0, i)),
            pl.BlockSpec((above.shape[0], block), lambda i: (0, i)),
            pl.BlockSpec((3, 2, block), lambda i: (0, 0, i)),
        ],
        out_specs=pl.BlockSpec((2, block, rows), lambda i: (0, i, 0)),
        out_shape=jax.ShapeDtypeStruct((2, width, rows), F32),
        compiler_params=params(SMALL_BYTES),
        cost_estimate=cost(16 * rows * width, 12 * rows * width),
        name="gate_mix",
    )(gates, below, above, taps)


def finish_kernel(gates_ref, conv_ref, out_ref):
    rows, block = out_ref.shape
    half = conv_ref.shape[1] // 2
    forward = conv_ref[:, :half].reshape(block, rows).astype(F32)
    reverse = conv_ref[:, half:].reshape(block, rows).astype(F32)
    out_ref[...] = (gates_ref[0] * forward + gates_ref[1] * reverse).T.astype(BF16)


def finish(gates, conv, block=256):
    _, width, rows = gates.shape
    block = min(block, width)
    pair = conv.shape[1]
    return pl.pallas_call(
        finish_kernel,
        grid=(width // block,),
        in_specs=[
            pl.BlockSpec((2, block, rows), lambda i: (0, i, 0)),
            pl.BlockSpec((2 * block // pair, pair, rows), lambda i: (i, 0, 0)),
        ],
        out_specs=pl.BlockSpec((rows, block), lambda i: (0, i)),
        out_shape=jax.ShapeDtypeStruct((rows, width), BF16),
        compiler_params=params(SMALL_BYTES),
        cost_estimate=cost(4 * rows * width, 14 * rows * width),
        name="finish",
    )(gates, conv)


def shards(tokens, in_weight, short_kernel, long_filter, skip_gain):
    ctx_count = lax.axis_size("ctx")
    tp_count = lax.axis_size("tp")
    rows, width = tokens.shape
    model = in_weight.shape[0]
    slice_width = width // ctx_count
    tiles = width // LANES
    t = tables(ctx_count, rows)

    def to_tp(x, bits):
        return lax.ppermute(x, "tp", [(i, i ^ bits) for i in range(tp_count)])

    def to_next(x):
        return lax.ppermute(x, "ctx", [(i, i + 1) for i in range(ctx_count - 1)])

    def to_previous(x):
        return lax.ppermute(x, "ctx", [(i + 1, i) for i in range(ctx_count - 1)])

    def exchange(x):
        return lax.all_to_all(x, "ctx", split_axis=0, concat_axis=0, tiled=True)

    weight_rows = in_weight.reshape(model, 2, tiles, LANES).transpose(0, 2, 1, 3).reshape(model * 2 * tiles, LANES)
    far = to_tp(tokens, 2)
    sib = to_tp(tokens, 1)
    filter_rows = filter_prep(long_filter).reshape(ctx_count, slice_width, rows)
    total, flat_far, flat_last = start_values(tokens, sib, weight_rows, width)
    far, filter_rows, total, flat_far, flat_last = lax.optimization_barrier(
        (far, filter_rows, total, flat_far, flat_last)
    )
    farsib = to_tp(far, 1)
    total = add_values(far, total, flat_far)
    values = add_values(farsib, total, flat_last, filter_rows)
    columns = exchange(values)
    parts, _ = lax.optimization_barrier(((tokens, sib, far, farsib), values))
    gates = project_gates(parts, weight_rows, width)
    below, above = to_next(gates[rows - 16 : rows]), to_previous(gates[rows : rows + 16])
    mixed = gate_mix(gates, below, above, short_kernel)
    columns, mixed = lax.optimization_barrier((columns, mixed))
    conv = exchange(convolve(columns, short_kernel, skip_gain[None], t))
    return finish(mixed, conv)


def solution(mesh):
    placed = (P("ctx", "tp"), P(None, None, "tp"), P(None, None, "tp"), P("ctx", "tp"), P("tp"))
    return jax.shard_map(shards, mesh=mesh, in_specs=placed, out_specs=P("ctx", "tp"), check_vma=False)
```

```python
import math

import jax
import jax.numpy as jnp
import numpy as np
from jax import lax
from jax.experimental import pallas as pl
from jax.experimental.pallas import tpu as pltpu
from jax.sharding import PartitionSpec as P

BF16 = jnp.bfloat16
F32 = jnp.float32
LANES = 128
GROUP = 8
PACK = 16
MIB = 1024 * 1024
PROJECT_BYTES = 50 * MIB
START_BYTES = 36 * MIB
END_BYTES = 20 * MIB
CONVOLVE_BYTES = 16 * MIB
SMALL_BYTES = 10 * MIB


def params(limit):
    return pltpu.CompilerParams(vmem_limit_bytes=limit)


def cost(flops, moved):
    return pl.CostEstimate(flops=flops, bytes_accessed=moved, transcendentals=0)


def mm(a, b):
    return jnp.dot(a, b, preferred_element_type=F32)


def tables(blocks, rows):
    length = blocks * rows
    half = rows // 2
    j1 = np.arange(blocks)
    q = np.arange(rows)
    outer = 2 * math.pi * ((4 * j1[:, None] + 1) * j1[None, :] % (4 * blocks)) / (4 * blocks)
    eye = np.eye(GROUP)
    forward = np.concatenate([np.kron(np.cos(outer), eye), np.kron(-np.sin(outer), eye)], 0)
    turn = 2 * math.pi * ((4 * j1[:, None] + 1) * q[None, :]) / (4 * length)
    turn = turn[:, None, :]
    inner = []
    for odd in (0, 1):
        angle = 2 * math.pi * (q[:half, None] * (2 * q[None, :half] + odd) % rows) / rows
        c, s = np.cos(angle), np.sin(angle)
        inner.append(np.block([[c, -s], [s, c]]))
    inner = np.stack(inner)
    small = lambda a: jnp.asarray(a.astype(np.float32)).astype(BF16)
    return dict(
        forward=small(forward),
        backward=small(forward.T),
        turn_cos=jnp.asarray(np.cos(turn), F32),
        turn_sin=jnp.asarray(np.sin(turn), F32),
        inner=small(inner),
        inner_back=small(inner.transpose(0, 2, 1) / length),
    )


def turns(cos_ref, sin_ref):
    blocks, _, rows = cos_ref.shape
    wide = lambda ref: jnp.broadcast_to(ref[...], (blocks, GROUP, rows)).reshape(blocks * GROUP, rows)
    return wide(cos_ref), wide(sin_ref)


def columns_of(x):
    blocks, _, rows = x.shape
    return [x[:, h * GROUP : (h + 1) * GROUP].reshape(blocks * GROUP, rows).astype(BF16) for h in range(2)]


def spectrum(xs, forward, turn_cos, turn_sin, inner):
    count, rows = xs[0].shape
    half = rows // 2
    near, far = [], []
    for x in xs:
        mixed = mm(forward, x)
        real, imag = mixed[:count], mixed[count:]
        turned = (real * turn_cos + imag * turn_sin, imag * turn_cos - real * turn_sin)
        near.append(jnp.concatenate([(t[:, :half] + t[:, half:]).astype(BF16) for t in turned], 1))
        far.append(jnp.concatenate([(t[:, :half] - t[:, half:]).astype(BF16) for t in turned], 1))
    return [mm(jnp.concatenate(parts, 0), inner[odd]) for odd, parts in enumerate((near, far))]


def filter_prep_kernel(filter_ref, out_ref):
    out_ref[...] = filter_ref[...].T.astype(BF16)


def filter_prep(long_filter, block=512):
    rows, width = long_filter.shape
    block = min(block, width)
    return pl.pallas_call(
        filter_prep_kernel,
        grid=(width // block,),
        in_specs=[pl.BlockSpec((rows, block), lambda i: (0, i))],
        out_specs=pl.BlockSpec((block, rows), lambda i: (i, 0)),
        out_shape=jax.ShapeDtypeStruct((width, rows), BF16),
        compiler_params=params(SMALL_BYTES),
        cost_estimate=cost(10 * rows * width, 6 * rows * width),
        name="filter_prep",
    )(long_filter)


def filter_spectrum(x, taps, skip, forward, turn_cos, turn_sin, inner):
    rows = x.shape[2]
    position = lax.broadcasted_iota(jnp.int32, (PACK, rows), 1)
    first = x[:1] + jnp.where(position == 0, skip, 0.0)[None]
    x = jnp.concatenate([first, x[1:]], 0)
    total = taps[0][None] * x
    for tap in (1, 2):
        moved = pltpu.roll(x, tap, 2)
        before = jnp.concatenate([jnp.zeros((1, PACK, rows), F32), moved[:-1]], 0)
        total = total + taps[tap][None] * jnp.where((position < tap)[None], before, moved)
    return spectrum(columns_of(total), forward, turn_cos, turn_sin, inner)


def convolve_kernel(
    taps_ref, skip_ref, forward_ref, cos_ref, sin_ref, inner_ref, inner_back_ref, backward_ref, x_hbm,
    out_ref, x_ref, spec_ref, sems
):
    blocks, width, rows = out_ref.shape
    half = rows // 2
    count = blocks * GROUP
    packs = width // PACK
    filter_packs = spec_ref.shape[0]
    order = [packs + p for p in range(filter_packs)] + list(range(packs))
    copies = {
        p: pltpu.make_async_copy(x_hbm.at[:, p * PACK : (p + 1) * PACK], x_ref.at[p], sems.at[p]) for p in order
    }
    for p in order:
        copies[p].start()
    turn_cos, turn_sin = turns(cos_ref, sin_ref)
    local = taps_ref.shape[2]
    columns = PACK * filter_packs
    lane = lax.broadcasted_iota(jnp.int32, (columns, local), 1)
    mine = lane - lax.broadcasted_iota(jnp.int32, (columns, local), 0) == lax.axis_index("ctx") * columns
    column = lambda row: jnp.sum(jnp.where(mine, row, 0.0), axis=1, keepdims=True)
    taps = [column(taps_ref[tap, 1:2]) for tap in range(3)]
    skip = column(skip_ref[...])
    for pack in range(filter_packs):
        these = slice(pack * PACK, (pack + 1) * PACK)
        copies[packs + pack].wait()
        x = x_ref[packs + pack].astype(F32)
        result = filter_spectrum(
            x, [t[these] for t in taps], skip[these], forward_ref[...], turn_cos, turn_sin, inner_ref
        )
        for odd in (0, 1):
            spec_ref[pack, odd] = result[odd]
    for pack in range(packs):
        copies[pack].wait()
        data = spectrum(columns_of(x_ref[pack].astype(F32)), forward_ref[...], turn_cos, turn_sin, inner_ref)
        back = []
        for odd in (0, 1):
            filt = spec_ref.at[pack % filter_packs, odd]
            real, imag = data[odd][:, :half], data[odd][:, half:]
            filter_real, filter_imag = filt[:, :half], filt[:, half:]
            if pack >= filter_packs:
                filter_imag = -filter_imag
            prod_real = (real * filter_real - imag * filter_imag).astype(BF16)
            prod_imag = (real * filter_imag + imag * filter_real).astype(BF16)
            back.append(mm(jnp.concatenate([prod_real, prod_imag], 1), inner_back_ref[odd]))
        outs = []
        for h in range(2):
            even, uneven = (part[h * count : (h + 1) * count] for part in back)
            near, far = even + uneven, even - uneven
            real = jnp.concatenate([near[:, :half], far[:, :half]], 1)
            imag = jnp.concatenate([near[:, half:], far[:, half:]], 1)
            turned_real = (real * turn_cos - imag * turn_sin).astype(BF16)
            turned_imag = (imag * turn_cos + real * turn_sin).astype(BF16)
            out = mm(backward_ref[...], jnp.concatenate([turned_real, turned_imag], 0))
            outs.append(out.reshape(blocks, GROUP, rows))
        out_ref[:, pack * PACK : (pack + 1) * PACK, :] = jnp.concatenate(outs, 1).astype(BF16)


def convolve(x, taps, skip, t):
    blocks, width, rows = x.shape
    count = width // 3
    vmem = pl.BlockSpec(memory_space=pltpu.VMEM)
    return pl.pallas_call(
        convolve_kernel,
        in_specs=[vmem] * 8 + [pl.BlockSpec(memory_space=pl.ANY)],
        out_specs=vmem,
        out_shape=jax.ShapeDtypeStruct((blocks, 2 * count, rows), BF16),
        scratch_shapes=[
            pltpu.VMEM((width // PACK, blocks, PACK, rows), BF16),
            pltpu.VMEM((count // PACK, 2, 2 * blocks * GROUP, rows), F32),
            pltpu.SemaphoreType.DMA((width // PACK,)),
        ],
        compiler_params=params(CONVOLVE_BYTES),
        cost_estimate=cost(5 * 10**9, 4 * MIB),
        name="convolve",
    )(taps, skip, t["forward"], t["turn_cos"], t["turn_sin"], t["inner"], t["inner_back"], t["backward"], x)


def swap_matrix(block):
    total = lax.broadcasted_iota(jnp.int32, (block, block), 0) + lax.broadcasted_iota(jnp.int32, (block, block), 1)
    return jnp.where(total == block - 1, 1.0, 0.0).astype(BF16)


def flip_into(dst, src, swap):
    block = swap.shape[0]
    count = src.shape[1] // block
    for b in range(count):
        piece = mm(src[:, (count - 1 - b) * block : (count - b) * block], swap)
        dst[:, b * block : (b + 1) * block] = piece.astype(BF16)


def picked(raw_ref, k, depth, width, first, count, which):
    tiles = width // LANES
    weights = [
        raw_ref[k, pl.ds(2 * tile + which, depth, stride=2 * tiles), :]
        for tile in range(first // LANES, (first + count) // LANES)
    ]
    return jnp.concatenate(weights, 1)


def weight_copies(w_hbm, raw_ref, sems):
    chunk = raw_ref.shape[1]
    tp = lax.axis_index("tp")
    return [
        pltpu.make_async_copy(
            w_hbm.at[pl.ds(pl.multiple_of((tp ^ k) * chunk, chunk), chunk)], raw_ref.at[k], sems.at[k]
        )
        for k in range(4)
    ]


def project_gates_kernel(
    own_hbm, sib_hbm, far_hbm, farsib_hbm, w_hbm, out_ref, left_ref, raw_ref, total_ref, part_sems, w_sems
):
    _, rows2, depth = left_ref.shape
    rows = rows2 // 2
    width = total_ref.shape[1]
    block = min(256, width)
    part_copies = [
        pltpu.make_async_copy(src, left_ref.at[k, :rows], part_sems.at[k])
        for k, src in enumerate((own_hbm, sib_hbm, far_hbm, farsib_hbm))
    ]
    w_copies = weight_copies(w_hbm, raw_ref, w_sems)
    w_copies[0].start()
    for copy in part_copies:
        copy.start()
    for copy in w_copies[1:]:
        copy.start()
    for copy in part_copies:
        copy.wait()
    swap = swap_matrix(block)
    for k in range(4):
        flip_into(left_ref.at[k, rows:], left_ref[3 - k, :rows], swap)
    for k in range(4):
        w_copies[k].wait()
        left = left_ref[k]
        for first in range(0, width, block):
            cols = slice(first, first + block)
            term = mm(left, picked(raw_ref, k, depth, width, first, block, 0))
            if k == 0:
                total_ref[:, cols] = term
            elif k < 3:
                total_ref[:, cols] += term
            else:
                out_ref[:, cols] = (total_ref[:, cols] + term).astype(BF16)


def project_gates(parts, weight_rows, width):
    rows, depth = parts[0].shape
    tiles = width // LANES
    model = weight_rows.shape[0] // (2 * tiles)
    return pl.pallas_call(
        project_gates_kernel,
        in_specs=[pl.BlockSpec(memory_space=pl.ANY)] * 5,
        out_specs=pl.BlockSpec(memory_space=pltpu.VMEM),
        scratch_shapes=[
            pltpu.VMEM((4, 2 * rows, depth), BF16),
            pltpu.VMEM((4, depth * 2 * tiles, LANES), BF16),
            pltpu.VMEM((2 * rows, width), F32),
            pltpu.SemaphoreType.DMA((4,)),
            pltpu.SemaphoreType.DMA((4,)),
        ],
        out_shape=jax.ShapeDtypeStruct((2 * rows, width), BF16),
        compiler_params=params(PROJECT_BYTES),
        cost_estimate=cost(4 * rows * model * width, 4 * model * width),
        name="project_gates",
    )(*parts, weight_rows)


def start_values_kernel(
    own_hbm, sib_hbm, w_hbm, total_ref, flat_far_hbm, flat_last_hbm, left_ref, raw_ref, flat_ref, part_sems, w_sems, flat_sems
):
    _, rows, depth = left_ref.shape
    width = total_ref.shape[1]
    block = min(256, width)
    part_copies = [
        pltpu.make_async_copy(src, left_ref.at[k], part_sems.at[k]) for k, src in enumerate((own_hbm, sib_hbm))
    ]
    w_copies = weight_copies(w_hbm, raw_ref, w_sems)
    flat_copies = [
        pltpu.make_async_copy(flat_ref.at[k], dst, flat_sems.at[k])
        for k, dst in enumerate((flat_last_hbm.at[1], flat_far_hbm.at[1], flat_far_hbm.at[0], flat_last_hbm.at[0]))
    ]
    w_copies[0].start()
    for copy in part_copies:
        copy.start()
    for copy in w_copies[1:]:
        copy.start()
    for copy in part_copies:
        copy.wait()
    swap = swap_matrix(block)
    for k in range(2):
        flip_into(left_ref.at[3 - k], left_ref[k], swap)
    for k in range(4):
        w_copies[k].wait()
        left = left_ref[k]
        here = slice(0, rows) if k < 2 else slice(rows, 2 * rows)
        for first in range(0, width, block):
            cols = slice(first, first + block)
            weights = picked(raw_ref, k, depth, width, first, block, 1)
            flat_ref[k, :, cols] = weights
            term = mm(left, weights)
            if k % 2 == 0:
                total_ref[here, cols] = term
            else:
                total_ref[here, cols] += term
        flat_copies[k].start()
    for copy in flat_copies:
        copy.wait()


def start_values(own, sib, weight_rows, width):
    rows, depth = own.shape
    tiles = width // LANES
    any_space = pl.BlockSpec(memory_space=pl.ANY)
    return pl.pallas_call(
        start_values_kernel,
        in_specs=[any_space] * 3,
        out_specs=[pl.BlockSpec(memory_space=pltpu.VMEM), any_space, any_space],
        scratch_shapes=[
            pltpu.VMEM((4, rows, depth), BF16),
            pltpu.VMEM((4, depth * 2 * tiles, LANES), BF16),
            pltpu.VMEM((4, depth, width), BF16),
            pltpu.SemaphoreType.DMA((2,)),
            pltpu.SemaphoreType.DMA((4,)),
            pltpu.SemaphoreType.DMA((4,)),
        ],
        out_shape=[
            jax.ShapeDtypeStruct((2 * rows, width), F32),
            jax.ShapeDtypeStruct((2, depth, width), BF16),
            jax.ShapeDtypeStruct((2, depth, width), BF16),
        ],
        compiler_params=params(START_BYTES),
        cost_estimate=cost(8 * rows * depth * width, 24 * depth * width),
        name="start_values",
    )(own, sib, weight_rows)


def add_values_kernel(last, part_ref, total_ref, flat_ref, *refs):
    if last:
        filter_hbm, out_hbm, left_ref, filter_sem, out_ref, out_sems = refs
        slice_width = filter_hbm.shape[1]
        filter_copy = pltpu.make_async_copy(filter_hbm, out_hbm.at[:, 2 * slice_width :], filter_sem)
        out_copies = []
    else:
        out_ref, left_ref = refs
    rows, depth = left_ref.shape
    width = total_ref.shape[1]
    block = min(256, width)
    if last:
        filter_copy.start()
    flip_into(left_ref, part_ref[...], swap_matrix(block))
    for strand in range(2):
        here = slice(strand * rows, (strand + 1) * rows)
        left = part_ref[...] if strand == 0 else left_ref[...]
        for b in range(width // block):
            cols = slice(b * block, (b + 1) * block)
            total = total_ref[here, cols] + mm(left, flat_ref[strand, :, cols])
            if last:
                turned = total.T.astype(BF16)
                per = block // slice_width
                for d in range(per):
                    out_ref[b * per + d, strand * slice_width : (strand + 1) * slice_width] = turned[
                        d * slice_width : (d + 1) * slice_width
                    ]
                where = (slice(b * per, (b + 1) * per), slice(strand * slice_width, (strand + 1) * slice_width))
                out_copies.append(
                    pltpu.make_async_copy(out_ref.at[where], out_hbm.at[where], out_sems.at[len(out_copies)])
                )
                out_copies[-1].start()
            else:
                out_ref[here, cols] = total
    if last:
        for copy in out_copies:
            copy.wait()
        filter_copy.wait()


def add_values(part, total, flat, filter_rows=None):
    rows, depth = part.shape
    width = total.shape[1]
    vmem = pl.BlockSpec(memory_space=pltpu.VMEM)
    any_space = pl.BlockSpec(memory_space=pl.ANY)
    last = filter_rows is not None
    extra = (filter_rows,) if last else ()
    if last:
        ctx_count, slice_width, _ = filter_rows.shape
        out_shape = jax.ShapeDtypeStruct((ctx_count, 3 * slice_width, rows), BF16)
        staging = [
            pltpu.SemaphoreType.DMA,
            pltpu.VMEM((ctx_count, 2 * slice_width, rows), BF16),
            pltpu.SemaphoreType.DMA((2 * width // min(256, width),)),
        ]
    else:
        out_shape = jax.ShapeDtypeStruct(total.shape, F32)
        staging = []

    def kernel(*refs):
        add_values_kernel(last, *refs)

    return pl.pallas_call(
        kernel,
        in_specs=[vmem] * 3 + [any_space] * len(extra),
        out_specs=any_space if last else vmem,
        scratch_shapes=[pltpu.VMEM((rows, depth), BF16)] + staging,
        out_shape=out_shape,
        compiler_params=params(END_BYTES),
        cost_estimate=cost(4 * rows * depth * width, 4 * depth * width),
        name="last_values" if last else "far_values",
    )(part, total, flat, *extra)


def gate_mix_kernel(gates_ref, below_ref, above_ref, taps_ref, out_ref):
    rows = gates_ref.shape[0] // 2
    block = gates_ref.shape[1]
    row = lax.broadcasted_iota(jnp.int32, (rows, block), 0)
    forward = gates_ref[:rows].astype(F32)
    reverse = gates_ref[rows:].astype(F32)
    below = below_ref[...].astype(F32)
    above = above_ref[...].astype(F32)
    tail = below.shape[0]
    gate_forward = taps_ref[0, 0:1] * forward
    gate_reverse = taps_ref[0, 0:1] * reverse
    for tap in (1, 2):
        moved = pltpu.roll(forward, tap, 0)
        other = pltpu.roll(reverse, rows - tap, 0)
        for edge in range(tap):
            moved = jnp.where(row == edge, below[tail - tap + edge : tail - tap + edge + 1], moved)
            other = jnp.where(row == rows - tap + edge, above[edge : edge + 1], other)
        gate_forward = gate_forward + taps_ref[tap, 0:1] * moved
        gate_reverse = gate_reverse + taps_ref[tap, 0:1] * other
    out_ref[0] = gate_forward.T
    out_ref[1] = gate_reverse.T


def gate_mix(gates, below, above, taps, block=256):
    rows, width = gates.shape[0] // 2, gates.shape[1]
    block = min(block, width)
    return pl.pallas_call(
        gate_mix_kernel,
        grid=(width // block,),
        in_specs=[
            pl.BlockSpec((2 * rows, block), lambda i: (0, i)),
            pl.BlockSpec((below.shape[0], block), lambda i: (0, i)),
            pl.BlockSpec((above.shape[0], block), lambda i: (0, i)),
            pl.BlockSpec((3, 2, block), lambda i: (0, 0, i)),
        ],
        out_specs=pl.BlockSpec((2, block, rows), lambda i: (0, i, 0)),
        out_shape=jax.ShapeDtypeStruct((2, width, rows), F32),
        compiler_params=params(SMALL_BYTES),
        cost_estimate=cost(16 * rows * width, 12 * rows * width),
        name="gate_mix",
    )(gates, below, above, taps)


def finish_kernel(gates_ref, conv_ref, out_ref):
    rows, block = out_ref.shape
    half = conv_ref.shape[1] // 2
    forward = conv_ref[:, :half].reshape(block, rows).astype(F32)
    reverse = conv_ref[:, half:].reshape(block, rows).astype(F32)
    out_ref[...] = (gates_ref[0] * forward + gates_ref[1] * reverse).T.astype(BF16)


def finish(gates, conv, block=256):
    _, width, rows = gates.shape
    block = min(block, width)
    pair = conv.shape[1]
    return pl.pallas_call(
        finish_kernel,
        grid=(width // block,),
        in_specs=[
            pl.BlockSpec((2, block, rows), lambda i: (0, i, 0)),
            pl.BlockSpec((2 * block // pair, pair, rows), lambda i: (i, 0, 0)),
        ],
        out_specs=pl.BlockSpec((rows, block), lambda i: (0, i)),
        out_shape=jax.ShapeDtypeStruct((rows, width), BF16),
        compiler_params=params(SMALL_BYTES),
        cost_estimate=cost(4 * rows * width, 14 * rows * width),
        name="finish",
    )(gates, conv)


def shards(tokens, in_weight, short_kernel, long_filter, skip_gain):
    ctx_count = lax.axis_size("ctx")
    tp_count = lax.axis_size("tp")
    rows, width = tokens.shape
    model = in_weight.shape[0]
    slice_width = width // ctx_count
    tiles = width // LANES
    t = tables(ctx_count, rows)

    def to_tp(x, bits):
        return lax.ppermute(x, "tp", [(i, i ^ bits) for i in range(tp_count)])

    def to_next(x):
        return lax.ppermute(x, "ctx", [(i, i + 1) for i in range(ctx_count - 1)])

    def to_previous(x):
        return lax.ppermute(x, "ctx", [(i + 1, i) for i in range(ctx_count - 1)])

    def exchange(x):
        return lax.all_to_all(x, "ctx", split_axis=0, concat_axis=0, tiled=True)

    weight_rows = in_weight.reshape(model, 2, tiles, LANES).transpose(0, 2, 1, 3).reshape(model * 2 * tiles, LANES)
    far = to_tp(tokens, 2)
    sib = to_tp(tokens, 1)
    filter_rows = filter_prep(long_filter).reshape(ctx_count, slice_width, rows)
    total, flat_far, flat_last = start_values(tokens, sib, weight_rows, width)
    far, filter_rows, total, flat_far, flat_last = lax.optimization_barrier(
        (far, filter_rows, total, flat_far, flat_last)
    )
    farsib = to_tp(far, 1)
    total = add_values(far, total, flat_far)
    values = add_values(farsib, total, flat_last, filter_rows)
    columns = exchange(values)
    parts, _ = lax.optimization_barrier(((tokens, sib, far, farsib), values))
    gates = project_gates(parts, weight_rows, width)
    below, above = to_next(gates[rows - 16 : rows]), to_previous(gates[rows : rows + 16])
    mixed = gate_mix(gates, below, above, short_kernel)
    columns, mixed = lax.optimization_barrier((columns, mixed))
    conv = exchange(convolve(columns, short_kernel, skip_gain[None], t))
    return finish(mixed, conv)


def solution(mesh):
    placed = (P("ctx", "tp"), P(None, None, "tp"), P(None, None, "tp"), P("ctx", "tp"), P("tp"))
    return jax.shard_map(shards, mesh=mesh, in_specs=placed, out_specs=P("ctx", "tp"), check_vma=False)
```
